256 devices in a mesh: mem: 8 (over x, core), state: 32 (over y, z).
Axes of the slice: x: 4, y: 4, z: 8, core: 2. Of those that a mesh axis runs over, the one named last changes fastest.
Arguments:
- prior_realizations: bfloat16 [64, 4, 2048, 512], P('mem', None, 'state'), may hold values from -6 to 6
- latent_stencil_weights: bfloat16 [128, 36], replicated, may hold values from -1 to 1
- latent_offset: float32 [128], replicated, may hold values from -3 to 3
- output_mixing_matrix: bfloat16 [4, 128], replicated, may hold values from -0.5 to 0.5
- transform: float32 [64, 64], replicated, may hold values from -0.35 to 1.35
- mean_weights: float32 [64], replicated, may hold values from -0.3 to 0.3
- obs_index: int32 [32, 8, 16], P('state', 'mem'), may hold values from 0 to 127, as said below
- obs_values: float32 [32, 8, 16, 128], P('state', 'mem'), may hold values from -6 to 6
- obs_precision: float32 [32, 8, 16, 128], P('state', 'mem'), may hold values from 0.083333333 to 3
Outputs:
- analysis: bfloat16 [64, 4, 2048, 512], P('mem', None, 'state')
- gram: float32 [64, 64], replicated
- proj: float32 [64], replicated
The draws below stay inside these ranges and needn't reach their ends.
Inputs may be any that keep to these rules, and one draw needn't show every extreme that they name: `obs_index`: in each device's list, entry j lies from j * 8 to (j + 1) * 8 - 1.
All inputs are finite; a program needn't handle non-finite values.
Results may differ from the reference program's by a relative error of at most 0.0053.
Values may be sent and summed in bfloat16 or wider, within the bound.
No kernel may reach another device: no remote copies, remote signals or barrier semaphores. Data moves between devices by JAX's collectives and lax.ppermute only.
A program may use at most 64 MiB of HBM per device.

```python
import math
import jax
import jax.numpy as jnp
from jax import lax

REALIZATIONS = 64
SITE_QUANTITIES = 4
HID = 128
PATCH_HEIGHT = 64
MESH_SPANWISE = 512
OBS_BLK = 16
PATCH_NUMBER = 32
SECTION_NUMBER = 8
NR = 2048
LANE_GROUPINGS = 128
OBS_TOTAL = 524288


def draw_transform(key, part):
    key = jax.random.fold_in(key, 3)
    entries = jnp.clip(jax.random.normal(key, (REALIZATIONS, REALIZATIONS), jnp.float32), -4.0, 4.0)
    entries = entries * (0.35 / jnp.sqrt(jnp.float32(REALIZATIONS)))
    return jnp.eye(REALIZATIONS, dtype=jnp.float32) + entries + entries.T


def draw_obs_index(key, part):
    key = jax.random.fold_in(key, 5)
    stride = LANE_GROUPINGS // OBS_BLK
    offsets = jax.random.randint(key, (PATCH_NUMBER, SECTION_NUMBER, OBS_BLK), 0, stride)
    return (jnp.arange(OBS_BLK, dtype=jnp.int32) * stride + offsets).astype(jnp.int32)


def draw_obs_precision(key, part):
    key = jax.random.fold_in(key, 7)
    grid_shape = (PATCH_NUMBER, SECTION_NUMBER, OBS_BLK, 128)
    rising = jnp.exp(jnp.log(3.0) * jnp.arange(PATCH_NUMBER, dtype=jnp.float32) / (PATCH_NUMBER - 1)).reshape(PATCH_NUMBER, 1, 1, 1)
    levels = jnp.exp(jax.random.uniform(key, grid_shape, jnp.float32, jnp.log(0.25), 0.0))
    return levels * rising


def steps_of(rng, dims, shards, least, largest):
    factor_of = 1.0
    for dim, shards_of in shards:
        draws = jax.random.uniform(jax.random.fold_in(jax.random.fold_in(rng, 6), dim), (shards_of,), jnp.float32, least / len(shards), largest / len(shards))
        factor_of = factor_of * jnp.repeat(jnp.exp(draws), dims[dim] // shards_of).reshape((-1,) + (1,) * (len(dims) - 1 - dim))
    return factor_of


def gaussian(stream_key, shape, scale, limit, shards=(), kind=jnp.bfloat16):
    drawn = scale * jax.random.normal(stream_key, shape, jnp.float32)
    if shards:
        drawn = drawn * steps_of(stream_key, shape, shards, -0.22, 0.18)
    return jnp.clip(drawn, -limit, limit).astype(kind)


def setup_inputs(seed: int = 0) -> dict:
    key_of = jax.random.split(jax.random.key(seed), 10)
    return {
        "prior_realizations": gaussian(key_of[0], (REALIZATIONS, SITE_QUANTITIES, NR, MESH_SPANWISE), 1.0, 6.0, ((0, 8), (2, 32))),
        "latent_stencil_weights": gaussian(key_of[1], (HID, 9 * SITE_QUANTITIES), (9 * SITE_QUANTITIES) ** -0.5, 1.0),
        "latent_offset": gaussian(key_of[2], (HID,), 0.5, 3.0, (), jnp.float32),
        "output_mixing_matrix": gaussian(key_of[3], (SITE_QUANTITIES, HID), HID ** -0.5, 0.5),
        "transform": draw_transform(jax.random.fold_in(key_of[9], 71), 0),
        "mean_weights": gaussian(key_of[5], (REALIZATIONS,), 0.05, 0.3, (), jnp.float32),
        "obs_index": draw_obs_index(jax.random.fold_in(key_of[9], 71), 0),
        "obs_values": gaussian(key_of[7], (PATCH_NUMBER, SECTION_NUMBER, OBS_BLK, 128), 1.0, 6.0, ((0, 32), (1, 8)), jnp.float32),
        "obs_precision": draw_obs_precision(jax.random.fold_in(key_of[9], 71), 0),
    }


def propagate_one_realization(realization_vector, latent_stencil_weights, latent_offset, output_mixing_matrix):
    row_count = realization_vector.shape[1]
    col_count = realization_vector.shape[2]
    bordered_vector = jnp.pad(realization_vector, ((0, 0), (1, 1), (1, 1)))
    patches = jnp.concatenate([bordered_vector[:, row_off:row_off + row_count, col_off:col_off + col_count] for row_off in range(3) for col_off in range(3)], axis=0)
    patches = patches.reshape(patches.shape[0], row_count * col_count)
    before = jnp.dot(latent_stencil_weights, patches, preferred_element_type=jnp.float32) + latent_offset[:, None]
    hidden = jax.nn.gelu(before, approximate=True).astype(jnp.bfloat16)
    increment = jnp.dot(output_mixing_matrix, hidden, preferred_element_type=jnp.float32)
    return (realization_vector.astype(jnp.float32) + increment.reshape(realization_vector.shape)).astype(jnp.bfloat16)

def reference(prior_realizations, latent_stencil_weights, latent_offset, output_mixing_matrix, transform, mean_weights, obs_index, obs_values, obs_precision):
    predicted_realizations = lax.map(lambda realization_vector: propagate_one_realization(realization_vector, latent_stencil_weights, latent_offset, output_mixing_matrix), prior_realizations)
    section_height = PATCH_HEIGHT // SECTION_NUMBER
    patch_sections = predicted_realizations.reshape(REALIZATIONS, SITE_QUANTITIES, PATCH_NUMBER, SECTION_NUMBER, section_height, MESH_SPANWISE).transpose(2, 3, 0, 1, 4, 5).reshape(PATCH_NUMBER, SECTION_NUMBER, REALIZATIONS, LANE_GROUPINGS, 128)
    picked = jax.vmap(jax.vmap(lambda tile_piece, places: jnp.take(tile_piece, places, axis=1)))(patch_sections, obs_index)
    observed = picked.astype(jnp.float32)
    obs_mean = lax.optimization_barrier(jnp.mean(observed, axis=2))
    spread = observed - obs_mean[:, :, None]
    weighted = spread * obs_precision[:, :, None]
    gram = jnp.einsum('smkbc,smjbc->kj', weighted, spread, precision=lax.Precision.HIGHEST) / OBS_TOTAL
    innovation = obs_precision * (obs_values - obs_mean)
    proj = jnp.einsum('smkbc,smbc->k', spread, innovation, precision=lax.Precision.HIGHEST) / math.sqrt(OBS_TOTAL)
    combined = transform + mean_weights[:, None]
    vector_patches = jnp.moveaxis(predicted_realizations.reshape(REALIZATIONS, SITE_QUANTITIES, PATCH_NUMBER, PATCH_HEIGHT * MESH_SPANWISE), 2, 0)

    def analyse(tile):
        realization_vectors = tile.reshape(REALIZATIONS, SITE_QUANTITIES * PATCH_HEIGHT * MESH_SPANWISE).astype(jnp.float32)
        state_mean = lax.optimization_barrier(jnp.mean(realization_vectors, axis=0))
        moved = state_mean + jnp.dot(combined.T, realization_vectors - state_mean, precision=lax.Precision.HIGHEST)
        return moved.astype(jnp.bfloat16).reshape(REALIZATIONS, SITE_QUANTITIES, PATCH_HEIGHT * MESH_SPANWISE)
    analysis = jnp.moveaxis(lax.map(analyse, vector_patches), 0, 2).reshape(REALIZATIONS, SITE_QUANTITIES, NR, MESH_SPANWISE)
    return (analysis, gram, proj)
```

```python
import functools
import math

import jax
import jax.numpy as jnp
import numpy as np
from jax import lax
from jax.experimental import pallas as pl
from jax.experimental.pallas import tpu as pltpu
from jax.sharding import PartitionSpec as P

BF = jnp.bfloat16
F32 = jnp.float32
VM = pltpu.VMEM
LIMIT = pltpu.CompilerParams(vmem_limit_bytes=56 * 1024 * 1024)

MEMBERS = 8
FIELDS = 4
ROWS = 64
COLS = 512
HID = 128
GROUP = 16
GROUPS = ROWS // GROUP
DEPTH = 224
CHUNKS = 4
LANES = 128
TILE = 256
GELU_A = math.sqrt(2.0 / math.pi)
GELU_B = GELU_A * 0.044715


def selection():
    chosen = np.zeros((DEPTH, GROUP, 39), np.float32)
    for b in range(3):
        for f in range(4):
            for row in range(GROUP):
                for a in (-1, 0, 1):
                    if 0 <= row + a < GROUP:
                        chosen[(b * 4 + f) * GROUP + row + a, row, (3 * (a + 1) + b) * 4 + f] = 1
            chosen[192 + b * 8 + f, 0, b * 4 + f] = 1
            chosen[196 + b * 8 + f, GROUP - 1, (6 + b) * 4 + f] = 1
    chosen[216:219, :, 36:] = np.eye(3)[:, None, :]
    return chosen.reshape(DEPTH * GROUP, 39)


def stencil_matrix(stencil, offset):
    half = 0.5 * offset
    cut = functools.partial(lax.reduce_precision, exponent_bits=8, mantissa_bits=7)
    first = cut(half)
    second = cut(half - first)
    third = half - first - second
    parts = jnp.stack([first, second, third], axis=1).astype(BF)
    rows = jnp.concatenate([(0.5 * stencil.astype(F32)).astype(BF), parts], axis=1)
    chosen = jnp.asarray(selection(), BF)
    spread = lax.dot_general(chosen, rows, (((1,), (1,)), ((), ())), preferred_element_type=F32)
    return spread.astype(BF).reshape(DEPTH, GROUP * HID)


def mixing_matrix(mixing):
    same = jnp.eye(GROUP, dtype=BF)
    return (mixing.T[None, :, :, None] * same[:, None, None, :]).reshape(GROUP * HID, 64)


def halved_gelu(half):
    return half + half * jnp.tanh(half * (8 * GELU_B * (half * half) + 2 * GELU_A))


def forecast_body(c, x_ref, edge_ref, w_ref, mix_ref, o_ref, p_ref, va, vb, ha, hb):
    lane = lax.broadcasted_iota(jnp.int32, (1, LANES), 1)
    row8 = lax.broadcasted_iota(jnp.int32, (8, LANES), 0)
    ones = jnp.where(row8 < 3, 1.0, 0.0).astype(F32)

    def three(read):
        mid = read(c)
        left = read(c - 1) if c > 0 else jnp.zeros_like(mid)
        right = read(c + 1) if c < CHUNKS - 1 else jnp.zeros_like(mid)
        return (
            jnp.where(lane == 0, pltpu.roll(left, 1, 1), pltpu.roll(mid, 1, 1)),
            mid,
            jnp.where(lane == LANES - 1, pltpu.roll(right, LANES - 1, 1), pltpu.roll(mid, LANES - 1, 1)),
        )

    def block(k, f, g, cc):
        return x_ref[k, f, g * 16 : (g + 1) * 16, cc * 128 : (cc + 1) * 128].astype(F32)

    def border(k, g, cc):
        edge = edge_ref[k, :, cc * 128 : (cc + 1) * 128]
        out = edge
        for f in range(FIELDS):
            if g > 0:
                out = jnp.where(row8 == f, pltpu.roll(block(k, f, g - 1, cc)[8:], (f + 1) % 8, 0), out)
            if g < GROUPS - 1:
                out = jnp.where(row8 == 4 + f, pltpu.roll(block(k, f, g + 1, cc)[:8], 4 + f, 0), out)
        return out

    def member(k, _):
        at = pl.ds(pl.multiple_of(k * LANES, LANES), LANES)
        for g in range(GROUPS):
            for f in range(FIELDS):
                for b, v in enumerate(three(lambda cc: block(k, f, g, cc))):
                    p_ref[g, (b * 4 + f) * 16 : (b * 4 + f + 1) * 16, at] = v.astype(BF)
            sides = three(lambda cc: border(k, g, cc))
            p_ref[g, 192:224, at] = jnp.concatenate([*sides, ones], axis=0).astype(BF)
        return 0

    lax.fori_loop(0, MEMBERS, member, 0)

    tiles = GROUP * HID // TILE
    held_v, held_h = (va, vb), (ha, hb)

    def group(g, _):
        patches = p_ref[g].T

        def before(n):
            held_v[n % 2][...] = jnp.dot(
                patches, w_ref[:, n * TILE : (n + 1) * TILE], preferred_element_type=F32
            )

        total = None
        before(0)
        for n in range(tiles + 1):
            if n + 1 < tiles:
                before(n + 1)
            if n < tiles:
                held_h[n % 2][...] = halved_gelu(held_v[n % 2][...]).astype(BF)
            if n >= 1:
                part = jnp.dot(
                    held_h[(n - 1) % 2][...],
                    mix_ref[(n - 1) * TILE : n * TILE, :],
                    preferred_element_type=F32,
                )
                total = part if total is None else total + part
        moved = total.T
        rows = pl.ds(pl.multiple_of(g * GROUP, GROUP), GROUP)
        for k in range(MEMBERS):
            new = [
                x_ref[k, f, rows, c * 128 : (c + 1) * 128].astype(F32)
                + moved[f * 16 : (f + 1) * 16, k * 128 : (k + 1) * 128]
                for f in range(FIELDS)
            ]
            for part in range(2):
                for pair in range(2):
                    both = [new[2 * pair + i][part * 8 : part * 8 + 8] for i in range(2)]
                    o_ref[2 * g + part, k, pair * 16 : pair * 16 + 16, :] = jnp.concatenate(
                        both, axis=0
                    ).astype(BF)
        return 0

    lax.fori_loop(0, GROUPS, group, 0)


def forecast_chunk(c, x, edges, weights, mix):
    cells = MEMBERS * LANES
    return pl.pallas_call(
        functools.partial(forecast_body, c),
        out_shape=jax.ShapeDtypeStruct((8, MEMBERS, 32, LANES), BF),
        in_specs=[pl.BlockSpec(memory_space=VM)] * 4,
        out_specs=pl.BlockSpec(memory_space=VM),
        scratch_shapes=[
            VM((GROUPS, DEPTH, cells), BF),
            VM((cells, TILE), F32),
            VM((cells, TILE), F32),
            VM((cells, TILE), BF),
            VM((cells, TILE), BF),
        ],
        compiler_params=LIMIT,
        name=f"forecast_{c}",
    )(x, edges, weights, mix)


def analysis_body(a_ref, f_ref, o_ref, s_ref, t_ref):
    s_ref[...] = f_ref[...].astype(F32).reshape(2048, LANES)
    for q in range(4):
        at = [pl.ds(q * 8 + i, 64, stride=32) for i in range(8)]
        states = jnp.concatenate([s_ref[i, :] for i in at], axis=1).astype(BF)
        both = jnp.dot(a_ref[...], states, preferred_element_type=F32)
        total = both[:64] + both[64:]
        for i in range(8):
            t_ref[at[i], :] = total[:, i * LANES : (i + 1) * LANES]
    o_ref[...] = t_ref[...].reshape(64, 32, LANES).astype(BF)


def analysis_chunk(update, states):
    return pl.pallas_call(
        analysis_body,
        out_shape=jax.ShapeDtypeStruct((64, 32, LANES), BF),
        in_specs=[pl.BlockSpec(memory_space=VM)] * 2,
        out_specs=pl.BlockSpec(memory_space=VM),
        scratch_shapes=[VM((2048, LANES), F32), VM((2048, LANES), F32)],
        compiler_params=LIMIT,
        name="analysis",
    )(update, states)


def gram_body(index_ref, values_ref, precision_ref, f0, f1, f2, f3, o_ref, s_ref, g_ref):
    for c, ref in enumerate((f0, f1, f2, f3)):
        s_ref[c * 2048 : (c + 1) * 2048, :] = ref[...].astype(F32).reshape(2048, LANES)
    for j in range(16):
        place = index_ref[j]
        start = lax.rem(place, 4) * 2048 + lax.div(place, 4)
        g_ref[:, j * LANES : (j + 1) * LANES] = s_ref[pl.ds(start, 64, stride=32), :]
    observed = g_ref[...]
    mean = jnp.sum(observed, axis=0, keepdims=True) * (1.0 / 64)
    spread = observed - mean
    weight = jnp.concatenate([precision_ref[j : j + 1, :] for j in range(16)], axis=1)
    value = jnp.concatenate([values_ref[j : j + 1, :] for j in range(16)], axis=1)
    weighted = spread * weight
    gram = lax.dot_general(
        spread,
        weighted,
        (((1,), (1,)), ((), ())),
        precision=lax.Precision.HIGHEST,
        preferred_element_type=F32,
    )
    proj = jnp.sum(weighted * (value - mean), axis=1, keepdims=True)
    o_ref[:, 0:64] = gram
    o_ref[:, 64:128] = jnp.broadcast_to(proj, (64, 64))


def gram_part(index, values, precision, chunks):
    return pl.pallas_call(
        gram_body,
        out_shape=jax.ShapeDtypeStruct((64, LANES), F32),
        in_specs=[pl.BlockSpec(memory_space=pltpu.SMEM)] + [pl.BlockSpec(memory_space=VM)] * 6,
        out_specs=pl.BlockSpec(memory_space=VM),
        scratch_shapes=[VM((4 * 2048, LANES), F32), VM((64, 2048), F32)],
        compiler_params=LIMIT,
        name="gram",
    )(index, values, precision, *chunks)


def place_body(c, *refs):
    b_ref, o_ref = refs[0], refs[-1]
    for k in range(MEMBERS):
        for pair in range(2):
            for half in range(4):
                low = b_ref[2 * half, k, pair * 16 : pair * 16 + 16, :].astype(F32)
                high = b_ref[2 * half + 1, k, pair * 16 : pair * 16 + 16, :].astype(F32)
                for i in range(2):
                    o_ref[k, 2 * pair + i, half * 16 : half * 16 + 16, :] = jnp.concatenate(
                        [low[i * 8 : i * 8 + 8], high[i * 8 : i * 8 + 8]], axis=0
                    ).astype(BF)


def place_chunk(c, back, so_far):
    first = so_far is None
    return pl.pallas_call(
        functools.partial(place_body, c),
        grid=(1,),
        out_shape=jax.ShapeDtypeStruct((MEMBERS, FIELDS, ROWS, COLS), BF),
        in_specs=[pl.BlockSpec((8, MEMBERS, 32, LANES), lambda i: (0, 0, 0, 0))]
        + ([] if first else [pl.BlockSpec(memory_space=pl.ANY)]),
        out_specs=pl.BlockSpec((MEMBERS, FIELDS, ROWS, LANES), lambda i: (0, 0, 0, c)),
        input_output_aliases={} if first else {1: 0},
        compiler_params=LIMIT,
        name=f"place_{c}",
    )(*([back] if first else [back, so_far]))


def sum_over(part, axis, groups=None):
    count = len(groups[0]) if groups else lax.axis_size(axis)
    copies = jnp.broadcast_to(part[None], (count, *part.shape))
    got = lax.all_to_all(
        copies, axis, split_axis=0, concat_axis=0, tiled=True, axis_index_groups=groups
    )
    return jnp.sum(got, axis=0)


def shards(
    prior_realizations,
    latent_stencil_weights,
    latent_offset,
    output_mixing_matrix,
    transform,
    mean_weights,
    obs_index,
    obs_values,
    obs_precision,
):
    count = lax.axis_size("state")
    forward = [(i, i + 1) for i in range(count - 1)]
    backward = [(i + 1, i) for i in range(count - 1)]
    low = lax.ppermute(prior_realizations[:, :, ROWS - 1, :], "state", forward)
    high = lax.ppermute(prior_realizations[:, :, 0, :], "state", backward)
    edges = jnp.concatenate([low, high], axis=1).astype(F32)

    weights = stencil_matrix(latent_stencil_weights, latent_offset)
    mix = mixing_matrix(output_mixing_matrix)
    combined = transform + mean_weights[:, None]
    update = (combined + (1.0 - jnp.sum(combined, axis=0)) / 64).T
    coarse = lax.reduce_precision(update, 8, 7)
    update = jnp.concatenate([coarse, update - coarse], axis=0).astype(BF)

    exchange = functools.partial(
        lax.all_to_all, axis_name="mem", split_axis=0, concat_axis=0, tiled=True
    )
    there = [
        exchange(forecast_chunk(c, prior_realizations, edges, weights, mix)) for c in range(CHUNKS)
    ]
    there = [piece.reshape(64, 32, LANES) for piece in there]
    back = [
        exchange(analysis_chunk(update, piece).reshape(8, MEMBERS, 32, LANES)) for piece in there
    ]
    part = gram_part(obs_index[0, 0], obs_values[0, 0], obs_precision[0, 0], there)
    total = sum_over(part, "mem")
    total = sum_over(total, "state", [[y * 8 + z for z in range(8)] for y in range(4)])
    total = sum_over(total, "state", [[y * 8 + z for y in range(4)] for z in range(8)])
    analysis = None
    for c in range(CHUNKS):
        analysis = place_chunk(c, back[c], analysis)
    gram = total[:, :64] / 524288
    proj = total[:, 64] / math.sqrt(524288)
    return (analysis, gram, proj)


def solution(mesh):
    return jax.shard_map(
        shards,
        mesh=mesh,
        in_specs=(
            P("mem", None, "state", None),
            P(),
            P(),
            P(),
            P(),
            P(),
            P("state", "mem", None),
            P("state", "mem", None, None),
            P("state", "mem", None, None),
        ),
        out_specs=(P("mem", None, "state", None), P(), P()),
        check_vma=False,
    )
```

```python
import functools
import math

import jax
import jax.numpy as jnp
from jax import lax
from jax.experimental import pallas as pl
from jax.experimental.pallas import tpu as pltpu
from jax.sharding import PartitionSpec as P

BF = jnp.bfloat16
F32 = jnp.float32
VM = pltpu.VMEM
LIMIT = pltpu.CompilerParams(vmem_limit_bytes=24 * 1024 * 1024)

MEMBERS = 8
FIELDS = 4
ROWS = 64
COLS = 512
HID = 128
GROUP = 16
GROUPS = ROWS // GROUP
DEPTH = 224
CHUNKS = 4
LANES = 128
TILE = 256
GELU_A = math.sqrt(2.0 / math.pi)
GELU_B = GELU_A * 0.044715


def held(x):
    return pltpu.with_memory_space_constraint(x, pltpu.VMEM)


def stored(x):
    return pltpu.with_memory_space_constraint(x, pltpu.HBM)


WHOLE = pl.BlockSpec(memory_space=VM)


def weights_body(rows_ref, mix_ref, w_ref, m_ref):
    k = lax.broadcasted_iota(jnp.int32, (DEPTH, LANES), 0)
    j = lax.broadcasted_iota(jnp.int32, (DEPTH, LANES), 1)
    b, f, row = k // 64, (k // 16) % 4, k % 16
    edge = k - 192
    edge_b, below, edge_f = edge // 8, (edge // 4) % 2, edge % 4
    lanes = lax.broadcasted_iota(jnp.int32, (HID, LANES), 1)
    linear = jnp.zeros((DEPTH, LANES), F32)
    for r in range(GROUP):
        inside = jnp.where(jnp.abs(row - r) <= 1, (3 * (row - r + 1) + b) * 4 + f, -1)
        border = (below * 6 + edge_b) * 4 + edge_f
        border = jnp.where(below * (GROUP - 1) == r, border, -1)
        want = jnp.where(k < 192, inside, jnp.where(k < 216, border, k - 180))
        chosen = jnp.where(j == want, 1.0, 0.0).astype(BF)
        part = jnp.dot(chosen, rows_ref[...], preferred_element_type=F32).astype(BF)
        w_ref[:, r * HID : (r + 1) * HID] = part
        spread = jnp.zeros((HID, LANES), F32)
        for field in range(FIELDS):
            spread = jnp.where(lanes == field * GROUP + r, mix_ref[:, field : field + 1], spread)
        spread = spread.astype(BF)
        m_ref[r * HID : (r + 1) * HID, :] = spread[:, :64]
        linear = linear + jnp.dot(part, spread, preferred_element_type=F32)
    linear = linear[:, :64]
    coarse = linear.astype(BF)
    w_ref[:, GROUP * HID :] = jnp.concatenate(
        [coarse, (linear - coarse.astype(F32)).astype(BF)], axis=1
    )


def product_weights(stencil, offset, mixing):
    half = 0.5 * offset
    cut = functools.partial(lax.reduce_precision, exponent_bits=8, mantissa_bits=7)
    first = cut(half)
    second = cut(half - first)
    third = half - first - second
    rows = jnp.concatenate(
        [0.5 * stencil.astype(F32).T, jnp.stack([first, second, third]), jnp.zeros((89, HID), F32)]
    ).astype(BF)
    return pl.pallas_call(
        weights_body,
        out_shape=(
            pltpu.HBM((DEPTH, GROUP * HID + LANES), BF),
            pltpu.HBM((GROUP * HID, 64), BF),
        ),
        in_specs=[WHOLE] * 2,
        out_specs=(WHOLE, WHOLE),
        compiler_params=LIMIT,
        name="weights",
    )(rows, mixing.astype(F32).T)


def forecast_body(chunks, columns, edge_ref, w_ref, mix_ref, *refs):
    windows, (o_ref, pa, pb, va, vb, ha, hb, s_ref) = refs[: len(columns)], refs[len(columns) :]
    windows = dict(zip(columns, windows))
    for slot, c in enumerate(chunks):
        forecast_block(
            c, slot, windows, edge_ref, w_ref, mix_ref, o_ref, pa, pb, va, vb, ha, hb, s_ref
        )


def forecast_block(
    c, slot, windows, edge_ref, w_ref, mix_ref, o_ref, pa, pb, va, vb, ha, hb, s_ref
):
    lane = lax.broadcasted_iota(jnp.int32, (1, LANES), 1)
    row8 = lax.broadcasted_iota(jnp.int32, (8, LANES), 0)
    ones = jnp.where(row8 < 3, 1.0, 0.0).astype(F32)

    def three(read):
        mid = read(c)
        left = read(c - 1) if c > 0 else jnp.zeros_like(mid)
        right = read(c + 1) if c < CHUNKS - 1 else jnp.zeros_like(mid)
        last = LANES - 1
        return (
            jnp.where(lane == 0, pltpu.roll(left, 1, 1), pltpu.roll(mid, 1, 1)),
            mid,
            jnp.where(lane == last, pltpu.roll(right, last, 1), pltpu.roll(mid, last, 1)),
        )

    def block(k, f, g, cc):
        rows = pl.ds(pl.multiple_of(g * GROUP, GROUP), GROUP)
        return windows[cc][k, f, rows, :].astype(F32)

    def border(k, g, cc):
        out = edge_ref[k, :, cc * LANES : (cc + 1) * LANES]
        above, below = jnp.maximum(g - 1, 0), jnp.minimum(g + 1, GROUPS - 1)
        for f in range(FIELDS):
            up = pltpu.roll(block(k, f, above, cc)[8:], (f + 1) % 8, 0)
            down = pltpu.roll(block(k, f, below, cc)[:8], 4 + f, 0)
            out = jnp.where((row8 == f) & (g > 0), up, out)
            out = jnp.where((row8 == 4 + f) & (g < GROUPS - 1), down, out)
        return out

    def build(g, k, to):
        inner = [three(lambda cc: block(k, f, g, cc)) for f in range(FIELDS)]
        parts = [inner[f][b] for b in range(3) for f in range(FIELDS)]
        parts += [*three(lambda cc: border(k, g, cc)), ones]
        to[k * LANES : (k + 1) * LANES, :] = jnp.concatenate(parts, axis=0).astype(BF).T

    tiles = GROUP * HID // TILE
    held_v, held_h = (va, vb), (ha, hb)

    def group(g, patches, following, to):
        def before(n):
            held_v[n % 2][...] = jnp.dot(
                patches[...], w_ref[:, n * TILE : (n + 1) * TILE], preferred_element_type=F32
            ).astype(BF)

        linear = jnp.dot(patches[...], w_ref[:, GROUP * HID :], preferred_element_type=F32)
        total = linear[:, :64] + linear[:, 64:]
        before(0)
        for n in range(tiles + 1):
            if n + 1 < tiles:
                before(n + 1)
            if n < tiles:
                h = held_v[n % 2][...]
                bend = jnp.tanh(h * (h * h * BF(8 * GELU_B) + BF(2 * GELU_A)))
                held_h[n % 2][...] = h * bend
                build(following, n, to)
            if n >= 1:
                total = total + jnp.dot(
                    held_h[(n - 1) % 2][...],
                    mix_ref[(n - 1) * TILE : n * TILE, :],
                    preferred_element_type=F32,
                )
        moved = total.T
        rows = pl.ds(pl.multiple_of(g * GROUP, GROUP), GROUP)
        for k in range(MEMBERS):
            new = [
                windows[c][k, f, rows, :].astype(F32)
                + moved[f * GROUP : (f + 1) * GROUP, k * LANES : (k + 1) * LANES]
                for f in range(FIELDS)
            ]
            for f in range(FIELDS):
                for part in range(2):
                    at = pl.ds(f * 64 + k, 8, stride=8)
                    s_ref[part, at, :] = new[f][part * 8 : part * 8 + 8]
        for part in range(2):
            o_ref[2 * g + part, slot] = s_ref[part].astype(BF)

    for k in range(MEMBERS):
        build(0, k, pa)

    def step(i, _):
        group(2 * i, pa, 2 * i + 1, pb)
        group(2 * i + 1, pb, jnp.minimum(2 * i + 2, GROUPS - 1), pa)
        return 0

    lax.fori_loop(0, GROUPS // 2, step, 0)


def forecast_chunks(chunks, x, edges, weights, mix):
    cells = MEMBERS * LANES
    count = len(chunks)
    columns = [c for c in range(CHUNKS) if chunks[0] - 1 <= c <= chunks[-1] + 1]
    shape = (MEMBERS, FIELDS, ROWS, LANES)
    return pl.pallas_call(
        functools.partial(forecast_body, chunks, columns),
        grid=(1,),
        out_shape=jax.ShapeDtypeStruct((8, count, 256, LANES), BF),
        in_specs=[WHOLE] * 3 + [pl.BlockSpec(shape, lambda i, c=c: (0, 0, 0, c)) for c in columns],
        out_specs=pl.BlockSpec((8, count, 256, LANES), lambda i: (0, 0, 0, 0)),
        scratch_shapes=[VM((cells, DEPTH), BF)] * 2
        + [VM((cells, TILE), BF)] * 4
        + [VM((2, 256, LANES), F32)],
        cost_estimate=pl.CostEstimate(
            flops=count * 10_000_000_000, bytes_accessed=4_000_000, transcendentals=0
        ),
        compiler_params=LIMIT,
        name=f"forecast_{chunks[0]}",
    )(edges, stored(weights), stored(mix), *[stored(x)] * len(columns))


def analysis_body(count, slots, a_ref, *refs):
    o_ref = refs[-1]
    for n in range(count):
        f_ref, slot = refs[n], slots[n]
        for q in range(4):
            spans = [slice((q * 8 + 2 * i) * 8, (q * 8 + 2 * i) * 8 + 16) for i in range(4)]
            got = [[f_ref[m, slot, span, :].astype(F32) for m in range(8)] for span in spans]
            rows = [
                jnp.concatenate([v[h * 8 : h * 8 + 8] for v in got[i]], axis=0)
                for i in range(4)
                for h in range(2)
            ]
            states = jnp.concatenate(rows, axis=1).astype(BF)
            both = jnp.dot(a_ref[...], states, preferred_element_type=F32)
            total = both[:64] + both[64:]
            for i, span in enumerate(spans):
                for m in range(8):
                    pair = [
                        total[m * 8 : m * 8 + 8, (2 * i + h) * LANES : (2 * i + h + 1) * LANES]
                        for h in range(2)
                    ]
                    o_ref[m, n, span, :] = jnp.concatenate(pair, axis=0).astype(BF)


def analysis_chunks(update, states, slots, buffer, to, total):
    count = len(slots)
    given = [update, *[held(s) for s in states]]
    alias = {}
    if buffer is not None:
        alias = {len(given): 0}
        given.append(buffer)
    return pl.pallas_call(
        functools.partial(analysis_body, count, slots),
        grid=(1,),
        out_shape=jax.ShapeDtypeStruct((8, total, 256, LANES), BF),
        in_specs=[WHOLE] * (1 + count) + [pl.BlockSpec(memory_space=pl.ANY)] * len(alias),
        out_specs=pl.BlockSpec((8, count, 256, LANES), lambda i: (0, to // count, 0, 0)),
        input_output_aliases=alias,
        compiler_params=LIMIT,
        name=f"analysis_{to}",
    )(*given)


def observed_rows(index_ref, chunks, g_ref):
    for j in range(16):
        place = index_ref[j]
        p = lax.div(place, 4)
        rows = pl.ds(pl.multiple_of(lax.div(p, 2) * 16, 16), 16)
        odd = lax.rem(p, 2) == 1
        for c, (ref, slot) in chunks.items():

            @pl.when(lax.rem(place, 4) == c)
            def _():
                for m in range(8):
                    two = ref[m, slot, rows, :].astype(F32)
                    g_ref[m * 8 : m * 8 + 8, j * LANES : (j + 1) * LANES] = jnp.where(
                        odd, two[8:], two[:8]
                    )


def gather_body(where, index_ref, *refs):
    o_ref = refs[-1]
    observed_rows(index_ref, {c: (refs[i], slot) for c, i, slot in where}, o_ref)


def gather_part(index, where, sources):
    return pl.pallas_call(
        functools.partial(gather_body, where),
        out_shape=jax.ShapeDtypeStruct((64, 2048), F32),
        in_specs=[pl.BlockSpec(memory_space=pltpu.SMEM)] + [WHOLE] * len(sources),
        out_specs=WHOLE,
        compiler_params=LIMIT,
        name="gather",
    )(index, *[held(s) for s in sources])


def gram_body(where, index_ref, values_ref, precision_ref, so_far_ref, f_ref, o_ref, g_ref):
    g_ref[...] = so_far_ref[...]
    observed_rows(index_ref, {c: (f_ref, slot) for c, slot in where}, g_ref)
    observed = g_ref[...]
    mean = jnp.sum(observed, axis=0, keepdims=True) * (1.0 / 64)
    spread = observed - mean
    weight = jnp.concatenate([precision_ref[j : j + 1, :] for j in range(16)], axis=1)
    value = jnp.concatenate([values_ref[j : j + 1, :] for j in range(16)], axis=1)
    dot = functools.partial(
        lax.dot_general,
        dimension_numbers=(((1,), (1,)), ((), ())),
        precision=lax.Precision.HIGHEST,
        preferred_element_type=F32,
    )
    gram = dot(spread * weight, spread)
    proj = dot(jnp.broadcast_to(weight * (value - mean), (8, 2048)), spread)
    o_ref[0:32, 0:64] = gram[:32]
    o_ref[0:32, 64:128] = gram[32:]
    o_ref[32:40, 0:64] = proj
    o_ref[32:40, 64:128] = proj


def gram_part(index, values, precision, so_far, where, states):
    return pl.pallas_call(
        functools.partial(gram_body, where),
        out_shape=jax.ShapeDtypeStruct((40, LANES), F32),
        in_specs=[pl.BlockSpec(memory_space=pltpu.SMEM)] + [WHOLE] * 4,
        out_specs=WHOLE,
        scratch_shapes=[VM((64, 2048), F32)],
        compiler_params=LIMIT,
        name="gram",
    )(index, values, precision, so_far, held(states))


def place_body(slots, *refs):
    o_ref, s_ref = refs[-2:]
    for i, (which, slot) in enumerate(slots):
        for m in range(8):
            s_ref[m] = refs[which][m, slot].astype(F32)
        for k in range(MEMBERS):
            for f in range(FIELDS):
                at = pl.ds(f * 64 + k, 8, stride=8)
                for half in range(4):
                    o_ref[
                        k, f, half * 16 : half * 16 + 16, i * LANES : (i + 1) * LANES
                    ] = jnp.concatenate(
                        [s_ref[2 * half, at, :], s_ref[2 * half + 1, at, :]], axis=0
                    ).astype(BF)


def place_chunks(at, sources, slots, so_far):
    given = [held(s) for s in sources]
    alias = {}
    if so_far is not None:
        alias[len(given)] = 0
        given.append(so_far)
    wide = len(slots) * LANES
    return pl.pallas_call(
        functools.partial(place_body, slots),
        grid=(1,),
        out_shape=jax.ShapeDtypeStruct((MEMBERS, FIELDS, ROWS, COLS), BF),
        in_specs=[WHOLE] * len(sources) + [pl.BlockSpec(memory_space=pl.ANY)] * len(alias),
        out_specs=pl.BlockSpec((MEMBERS, FIELDS, ROWS, wide), lambda i: (0, 0, 0, at)),
        scratch_shapes=[VM((8, 256, LANES), F32)],
        input_output_aliases=alias,
        compiler_params=LIMIT,
        name=f"place_{at}",
    )(*given)


def sum_over(part, axis, steps):
    size = lax.axis_size(axis)
    got = [lax.ppermute(part, axis, [(i, step(i)) for i in range(size)]) for step in steps]
    return functools.reduce(lambda a, b: a + b, got, part)


def shards(
    prior_realizations,
    latent_stencil_weights,
    latent_offset,
    output_mixing_matrix,
    transform,
    mean_weights,
    obs_index,
    obs_values,
    obs_precision,
):
    count = lax.axis_size("state")
    forward = [(i, i + 1) for i in range(count - 1)]
    backward = [(i + 1, i) for i in range(count - 1)]
    low = lax.ppermute(prior_realizations[:, :, ROWS - 1, :], "state", forward)
    high = lax.ppermute(prior_realizations[:, :, 0, :], "state", backward)
    edges = jnp.concatenate([low, high], axis=1).astype(F32)

    weights, mix = product_weights(latent_stencil_weights, latent_offset, output_mixing_matrix)
    combined = transform + mean_weights[:, None]
    update = (combined + (1.0 - jnp.sum(combined, axis=0)) / 64).T
    coarse = lax.reduce_precision(update, 8, 7)
    update = jnp.concatenate([coarse, update - coarse], axis=0).astype(BF)
    index = obs_index[0, 0]

    exchange = functools.partial(
        lax.all_to_all, axis_name="mem", split_axis=0, concat_axis=0, tiled=True
    )

    def forecast(chunks, edges):
        return forecast_chunks(chunks, prior_realizations, edges, weights, mix)

    x0 = exchange(forecast((0,), edges))
    x1 = exchange(forecast((1, 2), edges))
    x2 = exchange(forecast((3,), edges))
    held4 = analysis_chunks(update, [x0], [0], None, 0, 4)
    held4 = analysis_chunks(update, [x1], [0], held4, 1, 4)
    held4 = analysis_chunks(update, [x1], [1], held4, 2, 4)
    seen = gather_part(index, [(0, 0, 0), (1, 1, 0), (2, 1, 1)], [x0, x1])
    part = gram_part(index, obs_values[0, 0], obs_precision[0, 0], seen, [(3, 0)], x2)
    held4 = analysis_chunks(update, [x2], [0], held4, 3, 4)
    held4, total = lax.optimization_barrier((held4, part))
    x4 = exchange(held4)
    for n in (1, 2, 4):
        total = sum_over(total, "state", [lambda i: i ^ n])
    total = sum_over(total, "state", [lambda i, n=n: (i + 8 * n) % 32 for n in range(1, 4)])
    x4, total = lax.optimization_barrier((x4, total))
    total = jnp.sum(exchange(jnp.broadcast_to(total[None], (8, *total.shape))), axis=0)
    analysis = place_chunks(0, [x4], [(0, 0), (0, 1), (0, 2), (0, 3)], None)
    gram = jnp.concatenate([total[:32, :64], total[:32, 64:]], axis=0) / 524288
    proj = total[32, :64] / math.sqrt(524288)
    return (analysis, gram, proj)


def solution(mesh):
    return jax.shard_map(
        shards,
        mesh=mesh,
        in_specs=(
            P("mem", None, "state", None),
            P(),
            P(),
            P(),
            P(),
            P(),
            P("state", "mem", None),
            P("state", "mem", None, None),
            P("state", "mem", None, None),
        ),
        out_specs=(P("mem", None, "state", None), P(), P()),
        check_vma=False,
    )
```

```python
import functools
import math

import jax
import jax.numpy as jnp
from jax import lax
from jax.experimental import pallas as pl
from jax.experimental.pallas import tpu as pltpu
from jax.sharding import PartitionSpec as P

BF = jnp.bfloat16
F32 = jnp.float32
VM = pltpu.VMEM
LIMIT = pltpu.CompilerParams(vmem_limit_bytes=24 * 1024 * 1024)

MEMBERS = 8
FIELDS = 4
ROWS = 64
COLS = 512
HID = 128
GROUP = 16
GROUPS = ROWS // GROUP
DEPTH = 224
HOME_DEPTH = 128
CHUNKS = 4
RAW = 48
LANES = 128
TILE = 256
GELU_A = math.sqrt(2.0 / math.pi)
GELU_B = GELU_A * 0.044715


def held(x):
    return pltpu.with_memory_space_constraint(x, pltpu.VMEM)


def stored(x):
    return pltpu.with_memory_space_constraint(x, pltpu.HBM)


WHOLE = pl.BlockSpec(memory_space=VM)


def product_weights(height, rows, mixing, w_ref, m_ref):
    inner, depth = 12 * height, 12 * height + 32
    k = lax.broadcasted_iota(jnp.int32, (depth, LANES), 0)
    j = lax.broadcasted_iota(jnp.int32, (depth, LANES), 1)
    b, f, row = k // (4 * height), (k // height) % 4, k % height
    edge = k - inner
    edge_b, below, edge_f = edge // 8, (edge // 4) % 2, edge % 4
    lanes = lax.broadcasted_iota(jnp.int32, (HID, LANES), 1)
    linear = jnp.zeros((depth, LANES), F32)
    width = FIELDS * height
    for r in range(height):
        inside = jnp.where(jnp.abs(row - r) <= 1, (3 * (row - r + 1) + b) * 4 + f, -1)
        border = (below * 6 + edge_b) * 4 + edge_f
        border = jnp.where(below * (height - 1) == r, border, -1)
        want = jnp.where(k < inner, inside, jnp.where(edge < 24, border, edge + 12))
        chosen = jnp.where(j == want, 1.0, 0.0).astype(BF)
        part = jnp.dot(chosen, rows, preferred_element_type=F32).astype(BF)
        w_ref[:, r * HID : (r + 1) * HID] = part
        spread = jnp.zeros((HID, LANES), F32)
        for field in range(FIELDS):
            spread = jnp.where(lanes == field * height + r, mixing[:, field : field + 1], spread)
        spread = spread.astype(BF)
        m_ref[r * HID : (r + 1) * HID, :] = spread[:, :width]
        linear = linear + jnp.dot(part, spread, preferred_element_type=F32)
    linear = linear[:, :width]
    coarse = linear.astype(BF)
    fine = (linear - coarse.astype(F32)).astype(BF)
    w_ref[:, height * HID : height * HID + 2 * width] = jnp.concatenate([coarse, fine], axis=1)


def weights_body(
    stencil_ref, offset_ref, mixing_ref, transform_ref, mean_ref, w_ref, m_ref, hw_ref, hm_ref, u_ref
):
    stencil = 0.5 * stencil_ref[...].astype(F32)
    rows = jnp.concatenate([stencil, jnp.zeros((HID, LANES - 36), F32)], axis=1).T
    rest = 0.5 * offset_ref[...]
    for i in range(3):
        cut = rest.astype(BF).astype(F32)
        rest = rest - cut
        rows = jnp.where(lax.broadcasted_iota(jnp.int32, rows.shape, 0) == 36 + i, cut, rows)
    mixing = mixing_ref[...].astype(F32)
    mixing = jnp.concatenate([mixing, jnp.zeros((LANES - FIELDS, HID), F32)], axis=0).T
    product_weights(GROUP, rows.astype(BF), mixing, w_ref, m_ref)
    product_weights(8, rows.astype(BF), mixing, hw_ref, hm_ref)
    wide = jnp.concatenate([transform_ref[...], jnp.zeros((64, 64), F32)], axis=1)
    turned = jnp.concatenate([wide, jnp.zeros((64, LANES), F32)], axis=0).T[:64, :64]
    update = turned + mean_ref[...]
    update = update + (1.0 - jnp.sum(update, axis=1, keepdims=True)) * (1.0 / 64)
    coarse = update.astype(BF)
    u_ref[:64, :] = coarse
    u_ref[64:, :] = (update - coarse.astype(F32)).astype(BF)


def all_weights(stencil, offset, mixing, transform, mean_weights):
    return pl.pallas_call(
        weights_body,
        out_shape=(
            pltpu.HBM((DEPTH, GROUP * HID + LANES), BF),
            pltpu.HBM((GROUP * HID, 64), BF),
            pltpu.HBM((HOME_DEPTH, 8 * HID + LANES), BF),
            pltpu.HBM((8 * HID, 32), BF),
            pltpu.HBM((LANES, 64), BF),
        ),
        in_specs=[WHOLE] * 5,
        out_specs=(WHOLE,) * 5,
        compiler_params=LIMIT,
        name="weights",
    )(*map(stored, (stencil, offset[None], mixing, transform, mean_weights[None])))


def forecast_body(chunks, columns, raw, edge_ref, w_ref, mix_ref, *refs):
    windows, (o_ref, pa, pb, va, vb, ha, hb, s_ref) = refs[: len(columns)], refs[len(columns) :]
    windows = dict(zip(columns, windows))
    for slot, c in enumerate(chunks):
        forecast_block(
            c, slot, windows, raw, edge_ref, w_ref, mix_ref, o_ref, pa, pb, va, vb, ha, hb, s_ref
        )


def forecast_block(
    c, slot, windows, raw, edge_ref, w_ref, mix_ref, o_ref, pa, pb, va, vb, ha, hb, s_ref
):
    lane = lax.broadcasted_iota(jnp.int32, (1, LANES), 1)
    row8 = lax.broadcasted_iota(jnp.int32, (8, LANES), 0)
    ones = jnp.where(row8 < 3, 1.0, 0.0).astype(F32)

    def three(read):
        mid = read(c)
        left = read(c - 1) if c > 0 else jnp.zeros_like(mid)
        right = read(c + 1) if c < CHUNKS - 1 else jnp.zeros_like(mid)
        last = LANES - 1
        return (
            jnp.where(lane == 0, pltpu.roll(left, 1, 1), pltpu.roll(mid, 1, 1)),
            mid,
            jnp.where(lane == last, pltpu.roll(right, last, 1), pltpu.roll(mid, last, 1)),
        )

    def block(k, f, g, cc):
        rows = pl.ds(pl.multiple_of(g * GROUP, GROUP), GROUP)
        return windows[cc][k, f, rows, :].astype(F32)

    def border(k, g, cc):
        out = edge_ref[k, :, cc * LANES : (cc + 1) * LANES]
        above, below = jnp.maximum(g - 1, 0), jnp.minimum(g + 1, GROUPS - 1)
        for f in range(FIELDS):
            up = pltpu.roll(block(k, f, above, cc)[8:], (f + 1) % 8, 0)
            down = pltpu.roll(block(k, f, below, cc)[:8], 4 + f, 0)
            out = jnp.where((row8 == f) & (g > 0), up, out)
            out = jnp.where((row8 == 4 + f) & (g < GROUPS - 1), down, out)
        return out

    def build(g, k, to):
        inner = [three(lambda cc: block(k, f, g, cc)) for f in range(FIELDS)]
        parts = [inner[f][b] for b in range(3) for f in range(FIELDS)]
        parts += [*three(lambda cc: border(k, g, cc)), ones]
        to[k * LANES : (k + 1) * LANES, :] = jnp.concatenate(parts, axis=0).astype(BF).T

    def pack(g, k, part):
        last = CHUNKS - 1
        here = slice(part * 8, part * 8 + 8)
        above, below = jnp.maximum(g - 1, 0), jnp.minimum(g + 1, GROUPS - 1)

        def outer(cc):
            out = edge_ref[k, :, cc * LANES : (cc + 1) * LANES]
            for f in range(FIELDS):
                inner = block(k, f, g, cc)
                up = inner[:8] if part else block(k, f, above, cc)[8:]
                down = block(k, f, below, cc)[:8] if part else inner[8:]
                out = jnp.where((row8 == f) & (part + g > 0), pltpu.roll(up, (f + 1) % 8, 0), out)
                use = (row8 == 4 + f) & (g + part < GROUPS)
                out = jnp.where(use, pltpu.roll(down, 4 + f, 0), out)
            return out

        main = [block(k, f, g, last)[here] for f in range(FIELDS)]
        left = [block(k, f, g, last - 1)[here] for f in range(FIELDS)] + [outer(last - 1)]
        column = jnp.zeros((8, LANES), F32)
        for n, v in enumerate(left):
            column = jnp.where(lane == n, pltpu.roll(v, n + 1, 1), column)
        main += [outer(last), column]
        for i in range(3):
            o_ref[2 * g + part, 256 + k * RAW + i * 16 : 272 + k * RAW + i * 16, :] = (
                jnp.concatenate(main[2 * i : 2 * i + 2], axis=0).astype(BF)
            )

    tiles = GROUP * HID // TILE
    held_v, held_h = (va, vb), (ha, hb)

    def group(g, patches, following, to):
        def before(n):
            held_v[n % 2][...] = jnp.dot(
                patches[...], w_ref[:, n * TILE : (n + 1) * TILE], preferred_element_type=F32
            ).astype(BF)

        linear = jnp.dot(patches[...], w_ref[:, GROUP * HID :], preferred_element_type=F32)
        total = linear[:, :64] + linear[:, 64:]
        before(0)
        for n in range(tiles + 1):
            if n + 1 < tiles:
                before(n + 1)
            if n < tiles:
                h = held_v[n % 2][...]
                bend = jnp.tanh(h * (h * h * BF(8 * GELU_B) + BF(2 * GELU_A)))
                held_h[n % 2][...] = h * bend
                build(following, n, to)
                if raw:
                    pack(g, n, 0)
                    pack(g, n, 1)
            if n >= 1:
                total = total + jnp.dot(
                    held_h[(n - 1) % 2][...],
                    mix_ref[(n - 1) * TILE : n * TILE, :],
                    preferred_element_type=F32,
                )
        moved = total.T
        rows = pl.ds(pl.multiple_of(g * GROUP, GROUP), GROUP)
        for k in range(MEMBERS):
            new = [
                windows[c][k, f, rows, :].astype(F32)
                + moved[f * GROUP : (f + 1) * GROUP, k * LANES : (k + 1) * LANES]
                for f in range(FIELDS)
            ]
            for f in range(FIELDS):
                for part in range(2):
                    at = pl.ds(f * 64 + k, 8, stride=8)
                    s_ref[part, at, :] = new[f][part * 8 : part * 8 + 8]
        for part in range(2):
            o_ref[2 * g + part, slot * 256 : slot * 256 + 256, :] = s_ref[part].astype(BF)

    for k in range(MEMBERS):
        build(0, k, pa)

    def step(i, _):
        group(2 * i, pa, 2 * i + 1, pb)
        group(2 * i + 1, pb, jnp.minimum(2 * i + 2, GROUPS - 1), pa)
        return 0

    lax.fori_loop(0, GROUPS // 2, step, 0)


def forecast_chunks(chunks, raw, x, edges, weights, mix):
    cells = MEMBERS * LANES
    count = len(chunks)
    low, high = chunks[0] - 1, CHUNKS - 1 if raw else chunks[-1] + 1
    columns = [c for c in range(CHUNKS) if low <= c <= high]
    window = (MEMBERS, FIELDS, ROWS, LANES)
    shape = (8, count * 256 + raw * MEMBERS * RAW, LANES)
    return pl.pallas_call(
        functools.partial(forecast_body, chunks, columns, raw),
        grid=(1,),
        out_shape=jax.ShapeDtypeStruct(shape, BF),
        in_specs=[WHOLE] * 3 + [pl.BlockSpec(window, lambda i, c=c: (0, 0, 0, c)) for c in columns],
        out_specs=pl.BlockSpec(shape, lambda i: (0, 0, 0)),
        scratch_shapes=[VM((cells, DEPTH), BF)] * 2
        + [VM((cells, TILE), BF)] * 4
        + [VM((2, 256, LANES), F32)],
        cost_estimate=pl.CostEstimate(
            flops=count * 10_000_000_000, bytes_accessed=4_000_000, transcendentals=0
        ),
        compiler_params=LIMIT,
        name=f"forecast_{chunks[0]}",
    )(edges, stored(weights), stored(mix), *[stored(x)] * len(columns))


def home_body(x_ref, w_ref, mix_ref, o_ref, pa, pb, va, vb, ha, hb, s_ref):
    lane = lax.broadcasted_iota(jnp.int32, (1, LANES), 1)
    row8 = lax.broadcasted_iota(jnp.int32, (8, LANES), 0)
    ones = jnp.where(row8 < 3, 1.0, 0.0).astype(F32)
    last = LANES - 1

    def raw(m, k):
        got = [x_ref[m, 256 + k * RAW + i * 16 : 272 + k * RAW + i * 16, :] for i in range(3)]
        got = [v.astype(F32) for v in got]
        return [got[i // 2][i % 2 * 8 : i % 2 * 8 + 8] for i in range(6)]

    def build(m, k, to):
        *blocks, column = raw(m, k)
        three = []
        for n, mid in enumerate(blocks):
            first = pltpu.roll(column, (LANES - n) % LANES, 1)
            three.append(
                (
                    jnp.where(lane == 0, first, pltpu.roll(mid, 1, 1)),
                    mid,
                    jnp.where(lane == last, 0.0, pltpu.roll(mid, last, 1)),
                )
            )
        parts = [three[f][b] for b in range(3) for f in range(FIELDS)]
        parts += [*three[FIELDS], ones]
        to[k * LANES : (k + 1) * LANES, :] = jnp.concatenate(parts, axis=0).astype(BF).T

    tiles = 8 * HID // TILE
    held_v, held_h = (va, vb), (ha, hb)

    def group(m, patches, following, to):
        def before(n):
            held_v[n % 2][...] = jnp.dot(
                patches[...], w_ref[:, n * TILE : (n + 1) * TILE], preferred_element_type=F32
            ).astype(BF)

        linear = jnp.dot(patches[...], w_ref[:, 8 * HID :], preferred_element_type=F32)
        total = linear[:, :32] + linear[:, 32:64]
        before(0)
        for n in range(tiles + 1):
            if n + 1 < tiles:
                before(n + 1)
            if n < tiles:
                h = held_v[n % 2][...]
                bend = jnp.tanh(h * (h * h * BF(8 * GELU_B) + BF(2 * GELU_A)))
                held_h[n % 2][...] = h * bend
                build(following, 2 * n, to)
                build(following, 2 * n + 1, to)
            if n >= 1:
                total = total + jnp.dot(
                    held_h[(n - 1) % 2][...],
                    mix_ref[(n - 1) * TILE : n * TILE, :],
                    preferred_element_type=F32,
                )
        moved = total.T
        for k in range(MEMBERS):
            main = raw(m, k)
            for f in range(FIELDS):
                s_ref[pl.ds(f * 64 + k, 8, stride=8), :] = (
                    main[f] + moved[f * 8 : f * 8 + 8, k * LANES : (k + 1) * LANES]
                )
        o_ref[m] = s_ref[...].astype(BF)

    for k in range(MEMBERS):
        build(0, k, pa)

    def step(i, _):
        group(2 * i, pa, 2 * i + 1, pb)
        group(2 * i + 1, pb, jnp.minimum(2 * i + 2, 7), pa)
        return 0

    lax.fori_loop(0, 4, step, 0)


def home_forecast(states, weights, mix):
    cells = MEMBERS * LANES
    return pl.pallas_call(
        home_body,
        out_shape=jax.ShapeDtypeStruct((8, 256, LANES), BF),
        in_specs=[WHOLE] * 3,
        out_specs=WHOLE,
        scratch_shapes=[VM((cells, HOME_DEPTH), BF)] * 2
        + [VM((cells, TILE), BF)] * 4
        + [VM((256, LANES), F32)],
        cost_estimate=pl.CostEstimate(
            flops=10_000_000_000, bytes_accessed=4_000_000, transcendentals=0
        ),
        compiler_params=LIMIT,
        name="home",
    )(held(states), stored(weights), stored(mix))


def analysis_body(count, slots, a_ref, *refs):
    o_ref = refs[-1]
    for n in range(count):
        f_ref, slot = refs[n], slots[n]
        for q in range(4):
            spans = [slice((q * 8 + 2 * i) * 8, (q * 8 + 2 * i) * 8 + 16) for i in range(4)]
            got = [
                [f_ref[m, slot * 256 + span.start : slot * 256 + span.stop, :] for m in range(8)]
                for span in spans
            ]
            got = [[v.astype(F32) for v in vs] for vs in got]
            rows = [
                jnp.concatenate([v[h * 8 : h * 8 + 8] for v in got[i]], axis=0)
                for i in range(4)
                for h in range(2)
            ]
            states = jnp.concatenate(rows, axis=1).astype(BF)
            both = jnp.dot(a_ref[...], states, preferred_element_type=F32)
            total = both[:64] + both[64:]
            for i, span in enumerate(spans):
                for m in range(8):
                    pair = [
                        total[m * 8 : m * 8 + 8, (2 * i + h) * LANES : (2 * i + h + 1) * LANES]
                        for h in range(2)
                    ]
                    o_ref[m, n, span, :] = jnp.concatenate(pair, axis=0).astype(BF)


def analysis_chunks(update, states, slots, buffer, to, total):
    count = len(slots)
    given = [update, *[held(s) for s in states]]
    alias = {}
    if buffer is not None:
        alias = {len(given): 0}
        given.append(buffer)
    return pl.pallas_call(
        functools.partial(analysis_body, count, slots),
        grid=(1,),
        out_shape=jax.ShapeDtypeStruct((8, total, 256, LANES), BF),
        in_specs=[WHOLE] * (1 + count) + [pl.BlockSpec(memory_space=pl.ANY)] * len(alias),
        out_specs=pl.BlockSpec((8, count, 256, LANES), lambda i: (0, to // count, 0, 0)),
        input_output_aliases=alias,
        compiler_params=LIMIT,
        name=f"analysis_{to}",
    )(*given)


def observed_rows(index_ref, chunks, g_ref):
    for j in range(16):
        place = index_ref[j]
        p = lax.div(place, 4)
        odd = lax.rem(p, 2) == 1
        for c, (ref, slot) in chunks.items():

            @pl.when(lax.rem(place, 4) == c)
            def _():
                rows = pl.ds(pl.multiple_of(slot * 256 + lax.div(p, 2) * 16, 16), 16)
                for m in range(8):
                    two = ref[m, rows, :].astype(F32)
                    g_ref[m * 8 : m * 8 + 8, j * LANES : (j + 1) * LANES] = jnp.where(
                        odd, two[8:], two[:8]
                    )


def gram_body(where, index_ref, values_ref, precision_ref, *refs):
    o_ref, g_ref = refs[-2:]
    observed_rows(index_ref, {c: (refs[i], slot) for c, i, slot in where}, g_ref)
    observed = g_ref[...]
    mean = jnp.sum(observed, axis=0, keepdims=True) * (1.0 / 64)
    spread = observed - mean
    weight = jnp.concatenate([precision_ref[j : j + 1, :] for j in range(16)], axis=1)
    value = jnp.concatenate([values_ref[j : j + 1, :] for j in range(16)], axis=1)
    dot = functools.partial(
        lax.dot_general,
        dimension_numbers=(((1,), (1,)), ((), ())),
        precision=lax.Precision.HIGHEST,
        preferred_element_type=F32,
    )
    gram = dot(spread * weight, spread)
    proj = dot(jnp.broadcast_to(weight * (value - mean), (8, 2048)), spread)
    for n in range(8):
        o_ref[n, 0:32, 0:64] = gram[:32]
        o_ref[n, 0:32, 64:128] = gram[32:]
        o_ref[n, 32:40, 0:64] = proj
        o_ref[n, 32:40, 64:128] = proj


def gram_part(index, values, precision, where, sources):
    return pl.pallas_call(
        functools.partial(gram_body, where),
        out_shape=jax.ShapeDtypeStruct((8, 40, LANES), F32),
        in_specs=[pl.BlockSpec(memory_space=pltpu.SMEM)] + [WHOLE] * (2 + len(sources)),
        out_specs=WHOLE,
        scratch_shapes=[VM((64, 2048), F32)],
        compiler_params=LIMIT,
        name="gram",
    )(index, values, precision, *[held(s) for s in sources])


def place_body(slots, *refs):
    o_ref, s_ref = refs[-2:]
    for i, (which, slot) in enumerate(slots):
        for m in range(8):
            s_ref[m] = refs[which][m, slot].astype(F32)
        for k in range(MEMBERS):
            for f in range(FIELDS):
                at = pl.ds(f * 64 + k, 8, stride=8)
                for half in range(4):
                    o_ref[
                        k, f, half * 16 : half * 16 + 16, i * LANES : (i + 1) * LANES
                    ] = jnp.concatenate(
                        [s_ref[2 * half, at, :], s_ref[2 * half + 1, at, :]], axis=0
                    ).astype(BF)


def place_chunks(at, sources, slots, so_far):
    given = [held(s) for s in sources]
    alias = {}
    if so_far is not None:
        alias[len(given)] = 0
        given.append(so_far)
    wide = len(slots) * LANES
    return pl.pallas_call(
        functools.partial(place_body, slots),
        grid=(1,),
        out_shape=jax.ShapeDtypeStruct((MEMBERS, FIELDS, ROWS, COLS), BF),
        in_specs=[WHOLE] * len(sources) + [pl.BlockSpec(memory_space=pl.ANY)] * len(alias),
        out_specs=pl.BlockSpec((MEMBERS, FIELDS, ROWS, wide), lambda i: (0, 0, 0, at)),
        scratch_shapes=[VM((8, 256, LANES), F32)],
        input_output_aliases=alias,
        compiler_params=LIMIT,
        name=f"place_{at}",
    )(*given)


def sum_over(part, axis, steps):
    size = lax.axis_size(axis)
    got = [lax.ppermute(part, axis, [(i, step(i)) for i in range(size)]) for step in steps]
    return functools.reduce(lambda a, b: a + b, got, part)


def shards(
    prior_realizations,
    latent_stencil_weights,
    latent_offset,
    output_mixing_matrix,
    transform,
    mean_weights,
    obs_index,
    obs_values,
    obs_precision,
):
    count = lax.axis_size("state")
    forward = [(i, i + 1) for i in range(count - 1)]
    backward = [(i + 1, i) for i in range(count - 1)]
    low = lax.ppermute(prior_realizations[:, :, ROWS - 1, :], "state", forward)
    high = lax.ppermute(prior_realizations[:, :, 0, :], "state", backward)
    edges = jnp.concatenate([low, high], axis=1).astype(F32)

    weights, mix, home_weights, home_mix, update = all_weights(
        latent_stencil_weights, latent_offset, output_mixing_matrix, transform, mean_weights
    )
    index = obs_index[0, 0]

    exchange = functools.partial(
        lax.all_to_all, axis_name="mem", split_axis=0, concat_axis=0, tiled=True
    )

    def forecast(chunks, raw):
        return forecast_chunks(chunks, raw, prior_realizations, edges, weights, mix)

    x0 = exchange(forecast((0,), True))
    x1 = exchange(forecast((1, 2), False))
    x2 = home_forecast(x0, home_weights, home_mix)
    part = gram_part(
        index,
        obs_values[0, 0],
        obs_precision[0, 0],
        [(0, 0, 0), (1, 1, 0), (2, 1, 1), (3, 2, 0)],
        [x0, x1, x2],
    )
    total = jnp.sum(exchange(part), axis=0)
    held4 = analysis_chunks(update, [x0, x1, x1, x2], [0, 0, 1, 0], None, 0, 4)
    held4, total = lax.optimization_barrier((held4, total))
    x4 = exchange(held4)
    for n in (1, 2, 4, 8, 16):
        total = sum_over(total, "state", [lambda i, n=n: i ^ n])
    analysis = place_chunks(0, [x4], [(0, 0), (0, 1), (0, 2), (0, 3)], None)
    gram = jnp.concatenate([total[:32, :64], total[:32, 64:]], axis=0) / 524288
    proj = total[32, :64] / math.sqrt(524288)
    return (analysis, gram, proj)


def solution(mesh):
    return jax.shard_map(
        shards,
        mesh=mesh,
        in_specs=(
            P("mem", None, "state", None),
            P(),
            P(),
            P(),
            P(),
            P(),
            P("state", "mem", None),
            P("state", "mem", None, None),
            P("state", "mem", None, None),
        ),
        out_specs=(P("mem", None, "state", None), P(), P()),
        check_vma=False,
    )
```

```python
import functools
import math

import jax
import jax.numpy as jnp
from jax import lax
from jax.experimental import pallas as pl
from jax.experimental.pallas import tpu as pltpu
from jax.sharding import PartitionSpec as P

BF = jnp.bfloat16
F32 = jnp.float32
VM = pltpu.VMEM
LIMIT = pltpu.CompilerParams(vmem_limit_bytes=24 * 1024 * 1024)

MEMBERS = 8
FIELDS = 4
ROWS = 64
COLS = 512
HID = 128
GROUP = 16
GROUPS = ROWS // GROUP
DEPTH = 224
HOME_DEPTH = 128
CHUNKS = 4
RAW = 48
LANES = 128
TILE = 256
GELU_A = math.sqrt(2.0 / math.pi)
GELU_B = GELU_A * 0.044715


def held(x):
    return pltpu.with_memory_space_constraint(x, pltpu.VMEM)


def stored(x):
    return pltpu.with_memory_space_constraint(x, pltpu.HBM)


WHOLE = pl.BlockSpec(memory_space=VM)


def product_weights(height, rows, mixing, w_ref, m_ref):
    inner, depth = 12 * height, 12 * height + 32
    k = lax.broadcasted_iota(jnp.int32, (depth, LANES), 0)
    j = lax.broadcasted_iota(jnp.int32, (depth, LANES), 1)
    bits = height.bit_length() - 1
    b, f, row = k >> (bits + 2), (k >> bits) & 3, k & (height - 1)
    edge = k - inner
    edge_b, below, edge_f = edge >> 3, (edge >> 2) & 1, edge & 3
    lanes = lax.broadcasted_iota(jnp.int32, (HID, LANES), 1)
    linear = jnp.zeros((depth, LANES), F32)
    width = FIELDS * height
    for r in range(height):
        inside = jnp.where(jnp.abs(row - r) <= 1, (3 * (row - r + 1) + b) * 4 + f, -1)
        border = (below * 6 + edge_b) * 4 + edge_f
        border = jnp.where(below * (height - 1) == r, border, -1)
        want = jnp.where(k < inner, inside, jnp.where(edge < 24, border, edge + 12))
        chosen = jnp.where(j == want, 1.0, 0.0).astype(BF)
        part = jnp.dot(chosen, rows, preferred_element_type=F32).astype(BF)
        w_ref[:, r * HID : (r + 1) * HID] = part
        spread = jnp.zeros((HID, LANES), F32)
        for field in range(FIELDS):
            spread = jnp.where(lanes == field * height + r, mixing[:, field : field + 1], spread)
        spread = spread.astype(BF)
        m_ref[r * HID : (r + 1) * HID, :] = spread[:, :width]
        linear = linear + jnp.dot(part, spread, preferred_element_type=F32)
    linear = linear[:, :width]
    coarse = linear.astype(BF)
    fine = (linear - coarse.astype(F32)).astype(BF)
    w_ref[:, height * HID : height * HID + 2 * width] = jnp.concatenate([coarse, fine], axis=1)


def weights_body(
    stencil_ref,
    offset_ref,
    mixing_ref,
    transform_ref,
    mean_ref,
    w_ref,
    m_ref,
    hw_ref,
    hm_ref,
    u_ref,
    rows_ref,
):
    rows_ref[...] = jnp.zeros_like(rows_ref)
    rows_ref[:36, :] = 0.5 * stencil_ref[...].astype(F32)
    rows = rows_ref[...]
    rest = 0.5 * offset_ref[...]
    for i in range(3):
        cut = rest.astype(BF).astype(F32)
        rest = rest - cut
        rows = jnp.where(lax.broadcasted_iota(jnp.int32, rows.shape, 0) == 36 + i, cut, rows)
    mixing = mixing_ref[...].astype(F32)
    mixing = jnp.concatenate([mixing, jnp.zeros((LANES - FIELDS, HID), F32)], axis=0).T
    product_weights(GROUP, rows.astype(BF), mixing, w_ref, m_ref)
    product_weights(8, rows.astype(BF), mixing, hw_ref, hm_ref)
    wide = jnp.concatenate([transform_ref[...], jnp.zeros((64, 64), F32)], axis=1)
    turned = jnp.concatenate([wide, jnp.zeros((64, LANES), F32)], axis=0).T[:64, :64]
    update = turned + mean_ref[...]
    update = update + (1.0 - jnp.sum(update, axis=1, keepdims=True)) * (1.0 / 64)
    coarse = update.astype(BF)
    u_ref[:64, :] = coarse
    u_ref[64:, :] = (update - coarse.astype(F32)).astype(BF)


def all_weights(stencil, offset, mixing, transform, mean_weights):
    return pl.pallas_call(
        weights_body,
        out_shape=(
            pltpu.HBM((DEPTH, GROUP * HID + LANES), BF),
            pltpu.HBM((GROUP * HID, 64), BF),
            pltpu.HBM((HOME_DEPTH, 8 * HID + LANES), BF),
            pltpu.HBM((8 * HID, 32), BF),
            pltpu.HBM((LANES, 64), BF),
        ),
        in_specs=[WHOLE] * 5,
        out_specs=(WHOLE,) * 5,
        scratch_shapes=[VM((LANES, HID), F32)],
        compiler_params=LIMIT,
        name="weights",
    )(*map(stored, (stencil.T, offset[None], mixing, transform, mean_weights[None])))


def forecast_body(chunks, columns, raw, edge_ref, w_ref, mix_ref, x_ref, *refs):
    o_ref, pa, pb, va, vb, ha, hb, s_ref, window_ref, w_held, mix_held, sems = refs
    copies = [
        pltpu.make_async_copy(
            x_ref.at[:, :, :, c * LANES : (c + 1) * LANES], window_ref.at[i], sems.at[i]
        )
        for i, c in enumerate(columns)
    ]
    late = weight_copies(w_ref, mix_ref, w_held, mix_held, sems, len(columns))
    for copy in copies + late:
        copy.start()
    for copy in copies:
        copy.wait()
    windows = {c: window_ref.at[i] for i, c in enumerate(columns)}
    for slot, c in enumerate(chunks):
        forecast_block(
            c,
            slot,
            windows,
            raw,
            late if slot == 0 else [],
            edge_ref,
            w_held,
            mix_held,
            o_ref,
            pa,
            pb,
            va,
            vb,
            ha,
            hb,
            s_ref,
        )


def weight_copies(w_ref, mix_ref, w_held, mix_held, sems, at):
    return [
        pltpu.make_async_copy(w_ref, w_held, sems.at[at]),
        pltpu.make_async_copy(mix_ref, mix_held, sems.at[at + 1]),
    ]


def forecast_block(
    c,
    slot,
    windows,
    raw,
    late,
    edge_ref,
    w_ref,
    mix_ref,
    o_ref,
    pa,
    pb,
    va,
    vb,
    ha,
    hb,
    s_ref,
):
    lane = lax.broadcasted_iota(jnp.int32, (1, LANES), 1)
    row8 = lax.broadcasted_iota(jnp.int32, (8, LANES), 0)
    ones = jnp.where(row8 < 3, 1.0, 0.0).astype(F32)

    def three(read):
        mid = read(c)
        left = read(c - 1) if c > 0 else jnp.zeros_like(mid)
        right = read(c + 1) if c < CHUNKS - 1 else jnp.zeros_like(mid)
        last = LANES - 1
        return (
            pltpu.roll(jnp.where(lane == last, left, mid), 1, 1),
            mid,
            pltpu.roll(jnp.where(lane == 0, right, mid), last, 1),
        )

    def block(k, f, g, cc):
        rows = pl.ds(pl.multiple_of(g * GROUP, GROUP), GROUP)
        return windows[cc][k, f, rows, :].astype(F32)

    def border(k, g, cc):
        out = edge_ref[k, :, cc * LANES : (cc + 1) * LANES]
        above, below = jnp.maximum(g - 1, 0), jnp.minimum(g + 1, GROUPS - 1)
        for f in range(FIELDS):
            up = pltpu.roll(block(k, f, above, cc)[8:], (f + 1) % 8, 0)
            down = pltpu.roll(block(k, f, below, cc)[:8], 4 + f, 0)
            out = jnp.where((row8 == f) & (g > 0), up, out)
            out = jnp.where((row8 == 4 + f) & (g < GROUPS - 1), down, out)
        return out

    def build(g, k, to):
        inner = [three(lambda cc: block(k, f, g, cc)) for f in range(FIELDS)]
        parts = [inner[f][b] for b in range(3) for f in range(FIELDS)]
        parts += [*three(lambda cc: border(k, g, cc)), ones]
        to[k * LANES : (k + 1) * LANES, :] = jnp.concatenate(parts, axis=0).astype(BF).T

    def pack(g, k, part):
        last = CHUNKS - 1
        here = slice(part * 8, part * 8 + 8)
        above, below = jnp.maximum(g - 1, 0), jnp.minimum(g + 1, GROUPS - 1)

        def outer(cc):
            out = edge_ref[k, :, cc * LANES : (cc + 1) * LANES]
            for f in range(FIELDS):
                inner = block(k, f, g, cc)
                up = inner[:8] if part else block(k, f, above, cc)[8:]
                down = block(k, f, below, cc)[:8] if part else inner[8:]
                out = jnp.where((row8 == f) & (part + g > 0), pltpu.roll(up, (f + 1) % 8, 0), out)
                use = (row8 == 4 + f) & (g + part < GROUPS)
                out = jnp.where(use, pltpu.roll(down, 4 + f, 0), out)
            return out

        main = [block(k, f, g, last)[here] for f in range(FIELDS)]
        left = [block(k, f, g, last - 1)[here] for f in range(FIELDS)] + [outer(last - 1)]
        column = jnp.zeros((8, LANES), F32)
        for n, v in enumerate(left):
            column = jnp.where(lane == n, pltpu.roll(v, n + 1, 1), column)
        main += [outer(last), column]
        for i in range(3):
            o_ref[2 * g + part, 256 + k * RAW + i * 16 : 272 + k * RAW + i * 16, :] = (
                jnp.concatenate(main[2 * i : 2 * i + 2], axis=0).astype(BF)
            )

    tiles = GROUP * HID // TILE
    held_v, held_h = (va, vb), (ha, hb)

    def group(g, patches, following, to):
        def before(n):
            held_v[n % 2][...] = jnp.dot(
                patches[...], w_ref[:, n * TILE : (n + 1) * TILE], preferred_element_type=F32
            ).astype(BF)

        linear = jnp.dot(patches[...], w_ref[:, GROUP * HID :], preferred_element_type=F32)
        total = linear[:, :64] + linear[:, 64:]
        before(0)
        for n in range(tiles + 1):
            if n + 1 < tiles:
                before(n + 1)
            if n < tiles:
                h = held_v[n % 2][...]
                bend = jnp.tanh(h * (h * h * BF(8 * GELU_B) + BF(2 * GELU_A)))
                held_h[n % 2][...] = h * bend
                build(following, n, to)
                if raw:
                    pack(g, n, 0)
                    pack(g, n, 1)
            if n >= 1:
                total = total + jnp.dot(
                    held_h[(n - 1) % 2][...],
                    mix_ref[(n - 1) * TILE : n * TILE, :],
                    preferred_element_type=F32,
                )
        moved = total.T
        rows = pl.ds(pl.multiple_of(g * GROUP, GROUP), GROUP)
        for k in range(MEMBERS):
            new = [
                windows[c][k, f, rows, :].astype(F32)
                + moved[f * GROUP : (f + 1) * GROUP, k * LANES : (k + 1) * LANES]
                for f in range(FIELDS)
            ]
            for f in range(FIELDS):
                for part in range(2):
                    at = pl.ds(f * 64 + k, 8, stride=8)
                    s_ref[part, at, :] = new[f][part * 8 : part * 8 + 8]
        for part in range(2):
            o_ref[2 * g + part, slot * 256 : slot * 256 + 256, :] = s_ref[part].astype(BF)

    for k in range(MEMBERS):
        build(0, k, pa)
    for copy in late:
        copy.wait()

    def step(i, _):
        group(2 * i, pa, 2 * i + 1, pb)
        group(2 * i + 1, pb, jnp.minimum(2 * i + 2, GROUPS - 1), pa)
        return 0

    lax.fori_loop(0, GROUPS // 2, step, 0)


def forecast_chunks(chunks, raw, x, edges, weights, mix):
    cells = MEMBERS * LANES
    count = len(chunks)
    low, high = chunks[0] - 1, CHUNKS - 1 if raw else chunks[-1] + 1
    columns = [c for c in range(CHUNKS) if low <= c <= high]
    window = (len(columns), MEMBERS, FIELDS, ROWS, LANES)
    shape = (8, count * 256 + raw * MEMBERS * RAW, LANES)
    return pl.pallas_call(
        functools.partial(forecast_body, chunks, columns, raw),
        grid=(1,),
        out_shape=jax.ShapeDtypeStruct(shape, BF),
        in_specs=[WHOLE] + [pl.BlockSpec(memory_space=pl.ANY)] * 3,
        out_specs=pl.BlockSpec(shape, lambda i: (0, 0, 0)),
        scratch_shapes=[VM((cells, DEPTH), BF)] * 2
        + [VM((cells, TILE), BF)] * 4
        + [VM((2, 256, LANES), F32), VM(window, BF)]
        + [VM(weights.shape, BF), VM(mix.shape, BF)]
        + [pltpu.SemaphoreType.DMA((len(columns) + 2,))],
        cost_estimate=pl.CostEstimate(
            flops=count * 10_000_000_000, bytes_accessed=4_000_000, transcendentals=0
        ),
        compiler_params=LIMIT,
        name=f"forecast_{chunks[0]}",
    )(edges, stored(weights), stored(mix), stored(x))


def home_body(
    x_ref, w_given, mix_given, o_ref, pa, pb, va, vb, ha, hb, s_ref, w_ref, mix_ref, sems
):
    late = weight_copies(w_given, mix_given, w_ref, mix_ref, sems, 0)
    for copy in late:
        copy.start()
    lane = lax.broadcasted_iota(jnp.int32, (1, LANES), 1)
    row8 = lax.broadcasted_iota(jnp.int32, (8, LANES), 0)
    ones = jnp.where(row8 < 3, 1.0, 0.0).astype(F32)
    last = LANES - 1

    def raw(m, k):
        got = [x_ref[m, 256 + k * RAW + i * 16 : 272 + k * RAW + i * 16, :] for i in range(3)]
        got = [v.astype(F32) for v in got]
        return [got[i // 2][i % 2 * 8 : i % 2 * 8 + 8] for i in range(6)]

    def build(m, k, to):
        *blocks, column = raw(m, k)
        three = []
        for n, mid in enumerate(blocks):
            first = pltpu.roll(column, (LANES - n) % LANES, 1)
            three.append(
                (
                    jnp.where(lane == 0, first, pltpu.roll(mid, 1, 1)),
                    mid,
                    jnp.where(lane == last, 0.0, pltpu.roll(mid, last, 1)),
                )
            )
        parts = [three[f][b] for b in range(3) for f in range(FIELDS)]
        parts += [*three[FIELDS], ones]
        to[k * LANES : (k + 1) * LANES, :] = jnp.concatenate(parts, axis=0).astype(BF).T

    tiles = 8 * HID // TILE
    held_v, held_h = (va, vb), (ha, hb)

    def group(m, patches, following, to):
        def before(n):
            held_v[n % 2][...] = jnp.dot(
                patches[...], w_ref[:, n * TILE : (n + 1) * TILE], preferred_element_type=F32
            ).astype(BF)

        linear = jnp.dot(patches[...], w_ref[:, 8 * HID :], preferred_element_type=F32)
        total = linear[:, :32] + linear[:, 32:64]
        before(0)
        for n in range(tiles + 1):
            if n + 1 < tiles:
                before(n + 1)
            if n < tiles:
                h = held_v[n % 2][...]
                bend = jnp.tanh(h * (h * h * BF(8 * GELU_B) + BF(2 * GELU_A)))
                held_h[n % 2][...] = h * bend
                build(following, 2 * n, to)
                build(following, 2 * n + 1, to)
            if n >= 1:
                total = total + jnp.dot(
                    held_h[(n - 1) % 2][...],
                    mix_ref[(n - 1) * TILE : n * TILE, :],
                    preferred_element_type=F32,
                )
        moved = total.T
        for k in range(MEMBERS):
            main = raw(m, k)
            for f in range(FIELDS):
                s_ref[pl.ds(f * 64 + k, 8, stride=8), :] = (
                    main[f] + moved[f * 8 : f * 8 + 8, k * LANES : (k + 1) * LANES]
                )
        o_ref[m] = s_ref[...].astype(BF)

    for k in range(MEMBERS):
        build(0, k, pa)
    for copy in late:
        copy.wait()

    def step(i, _):
        group(2 * i, pa, 2 * i + 1, pb)
        group(2 * i + 1, pb, jnp.minimum(2 * i + 2, 7), pa)
        return 0

    lax.fori_loop(0, 4, step, 0)


def home_forecast(states, weights, mix):
    cells = MEMBERS * LANES
    return pl.pallas_call(
        home_body,
        out_shape=jax.ShapeDtypeStruct((8, 256, LANES), BF),
        in_specs=[WHOLE] + [pl.BlockSpec(memory_space=pl.ANY)] * 2,
        out_specs=WHOLE,
        scratch_shapes=[VM((cells, HOME_DEPTH), BF)] * 2
        + [VM((cells, TILE), BF)] * 4
        + [VM((256, LANES), F32), VM(weights.shape, BF), VM(mix.shape, BF)]
        + [pltpu.SemaphoreType.DMA((2,))],
        cost_estimate=pl.CostEstimate(
            flops=10_000_000_000, bytes_accessed=4_000_000, transcendentals=0
        ),
        compiler_params=LIMIT,
        name="home",
    )(held(states), stored(weights), stored(mix))


def analysis_body(count, slots, a_ref, *refs):
    o_ref = refs[-1]
    for n in range(count):
        f_ref, slot = refs[n], slots[n]
        for q in range(4):
            spans = [slice((q * 8 + 2 * i) * 8, (q * 8 + 2 * i) * 8 + 16) for i in range(4)]
            got = [
                [f_ref[m, slot * 256 + span.start : slot * 256 + span.stop, :] for m in range(8)]
                for span in spans
            ]
            got = [[v.astype(F32) for v in vs] for vs in got]
            rows = [
                jnp.concatenate([v[h * 8 : h * 8 + 8] for v in got[i]], axis=0)
                for i in range(4)
                for h in range(2)
            ]
            states = jnp.concatenate(rows, axis=1).astype(BF)
            both = jnp.dot(a_ref[...], states, preferred_element_type=F32)
            total = both[:64] + both[64:]
            for i, span in enumerate(spans):
                for m in range(8):
                    pair = [
                        total[m * 8 : m * 8 + 8, (2 * i + h) * LANES : (2 * i + h + 1) * LANES]
                        for h in range(2)
                    ]
                    o_ref[m, n, span, :] = jnp.concatenate(pair, axis=0).astype(BF)


def analysis_chunks(update, states, slots, buffer, to, total):
    count = len(slots)
    given = [update, *[held(s) for s in states]]
    alias = {}
    if buffer is not None:
        alias = {len(given): 0}
        given.append(buffer)
    return pl.pallas_call(
        functools.partial(analysis_body, count, slots),
        grid=(1,),
        out_shape=jax.ShapeDtypeStruct((8, total, 256, LANES), BF),
        in_specs=[WHOLE] * (1 + count) + [pl.BlockSpec(memory_space=pl.ANY)] * len(alias),
        out_specs=pl.BlockSpec((8, count, 256, LANES), lambda i: (0, to // count, 0, 0)),
        input_output_aliases=alias,
        compiler_params=LIMIT,
        name=f"analysis_{to}",
    )(*given)


def observed_rows(index_ref, chunks, g_ref):
    for j in range(16):
        place = index_ref[j]
        p = lax.div(place, 4)
        odd = lax.rem(p, 2) == 1
        for c, (ref, slot) in chunks.items():

            @pl.when(lax.rem(place, 4) == c)
            def _():
                rows = pl.ds(pl.multiple_of(slot * 256 + lax.div(p, 2) * 16, 16), 16)
                for m in range(8):
                    two = ref[m, rows, :].astype(F32)
                    g_ref[m * 8 : m * 8 + 8, j * LANES : (j + 1) * LANES] = jnp.where(
                        odd, two[8:], two[:8]
                    )


def in_two(v):
    coarse = v.astype(BF)
    return coarse, (v - coarse.astype(F32)).astype(BF)


def gram_body(where, index_ref, values_ref, precision_ref, *refs):
    o_ref, g_ref = refs[-2:]
    observed_rows(index_ref, {c: (refs[i], slot) for c, i, slot in where}, g_ref)
    observed = g_ref[...]
    mean = jnp.sum(observed, axis=0, keepdims=True) * (1.0 / 64)
    spread = observed - mean
    weight = jnp.concatenate([precision_ref[j : j + 1, :] for j in range(16)], axis=1)
    value = jnp.concatenate([values_ref[j : j + 1, :] for j in range(16)], axis=1)
    left = jnp.broadcast_to(weight * (value - mean), (8, 2048))
    left = jnp.concatenate([spread * weight, left], axis=0)
    left, left_rest = in_two(left)
    right, right_rest = in_two(spread)
    both = lax.dot_general(
        jnp.concatenate([left, left, left_rest], axis=1),
        jnp.concatenate([right, right_rest, right], axis=1),
        (((1,), (1,)), ((), ())),
        preferred_element_type=F32,
    )
    gram, proj = both[:64], both[64:]
    for n in range(8):
        o_ref[n, 0:32, 0:64] = gram[:32]
        o_ref[n, 0:32, 64:128] = gram[32:]
        o_ref[n, 32:40, 0:64] = proj
        o_ref[n, 32:40, 64:128] = proj


def gram_part(index, values, precision, where, sources):
    return pl.pallas_call(
        functools.partial(gram_body, where),
        out_shape=jax.ShapeDtypeStruct((8, 40, LANES), F32),
        in_specs=[pl.BlockSpec(memory_space=pltpu.SMEM)] + [WHOLE] * (2 + len(sources)),
        out_specs=WHOLE,
        scratch_shapes=[VM((64, 2048), F32)],
        compiler_params=LIMIT,
        name="gram",
    )(index, values, precision, *[held(s) for s in sources])


def place_body(slots, *refs):
    o_ref, s_ref = refs[-2:]
    for i, (which, slot) in enumerate(slots):
        for m in range(8):
            s_ref[m] = refs[which][m, slot].astype(F32)
        for k in range(MEMBERS):
            for f in range(FIELDS):
                at = pl.ds(f * 64 + k, 8, stride=8)
                for half in range(4):
                    o_ref[
                        k, f, half * 16 : half * 16 + 16, i * LANES : (i + 1) * LANES
                    ] = jnp.concatenate(
                        [s_ref[2 * half, at, :], s_ref[2 * half + 1, at, :]], axis=0
                    ).astype(BF)


def place_chunks(at, sources, slots, so_far):
    given = [held(s) for s in sources]
    alias = {}
    if so_far is not None:
        alias[len(given)] = 0
        given.append(so_far)
    wide = len(slots) * LANES
    return pl.pallas_call(
        functools.partial(place_body, slots),
        grid=(1,),
        out_shape=jax.ShapeDtypeStruct((MEMBERS, FIELDS, ROWS, COLS), BF),
        in_specs=[WHOLE] * len(sources) + [pl.BlockSpec(memory_space=pl.ANY)] * len(alias),
        out_specs=pl.BlockSpec((MEMBERS, FIELDS, ROWS, wide), lambda i: (0, 0, 0, at)),
        scratch_shapes=[VM((8, 256, LANES), F32)],
        input_output_aliases=alias,
        compiler_params=LIMIT,
        name=f"place_{at}",
    )(*given)


def sum_over(part, axis, steps):
    size = lax.axis_size(axis)
    got = [lax.ppermute(part, axis, [(i, step(i)) for i in range(size)]) for step in steps]
    return functools.reduce(lambda a, b: a + b, got, part)


def shards(
    prior_realizations,
    latent_stencil_weights,
    latent_offset,
    output_mixing_matrix,
    transform,
    mean_weights,
    obs_index,
    obs_values,
    obs_precision,
):
    count = lax.axis_size("state")
    forward = [(i, i + 1) for i in range(count - 1)]
    backward = [(i + 1, i) for i in range(count - 1)]
    low = lax.ppermute(prior_realizations[:, :, ROWS - 1, :], "state", forward)
    high = lax.ppermute(prior_realizations[:, :, 0, :], "state", backward)
    edges = jnp.concatenate([low, high], axis=1).astype(F32)

    weights, mix, home_weights, home_mix, update = all_weights(
        latent_stencil_weights, latent_offset, output_mixing_matrix, transform, mean_weights
    )
    index = obs_index[0, 0]

    exchange = functools.partial(
        lax.all_to_all, axis_name="mem", split_axis=0, concat_axis=0, tiled=True
    )

    def forecast(chunks, raw):
        return forecast_chunks(chunks, raw, prior_realizations, edges, weights, mix)

    x0 = exchange(forecast((0,), True))
    x1 = exchange(forecast((1, 2), False))
    x2 = home_forecast(x0, home_weights, home_mix)
    part = gram_part(
        index,
        obs_values[0, 0],
        obs_precision[0, 0],
        [(0, 0, 0), (1, 1, 0), (2, 1, 1), (3, 2, 0)],
        [x0, x1, x2],
    )
    total = jnp.sum(exchange(part), axis=0)
    held4 = analysis_chunks(update, [x0, x1, x1, x2], [0, 0, 1, 0], None, 0, 4)
    held4, total = lax.optimization_barrier((held4, total))
    x4 = exchange(held4)
    for n in (1, 2, 4, 8, 16):
        total = sum_over(total, "state", [lambda i, n=n: i ^ n])
    analysis = place_chunks(0, [x4], [(0, 0), (0, 1), (0, 2), (0, 3)], None)
    gram = jnp.concatenate([total[:32, :64], total[:32, 64:]], axis=0) / 524288
    proj = total[32, :64] / math.sqrt(524288)
    return (analysis, gram, proj)


def solution(mesh):
    return jax.shard_map(
        shards,
        mesh=mesh,
        in_specs=(
            P("mem", None, "state", None),
            P(),
            P(),
            P(),
            P(),
            P(),
            P("state", "mem", None),
            P("state", "mem", None, None),
            P("state", "mem", None, None),
        ),
        out_specs=(P("mem", None, "state", None), P(), P()),
        check_vma=False,
    )
```

```python
import functools
import math

import jax
import jax.numpy as jnp
from jax import lax
from jax.experimental import pallas as pl
from jax.experimental.pallas import tpu as pltpu
from jax.sharding import PartitionSpec as P

BF = jnp.bfloat16
F32 = jnp.float32
VM = pltpu.VMEM
LIMIT = pltpu.CompilerParams(vmem_limit_bytes=24 * 1024 * 1024)

MEMBERS = 8
FIELDS = 4
ROWS = 64
COLS = 512
HID = 128
GROUP = 16
GROUPS = ROWS // GROUP
DEPTH = 224
HOME_DEPTH = 128
CHUNKS = 4
OBSERVED = 32 * 8 * 16 * 128
RAW = 48
LANES = 128
TILE = 256
GELU_A = math.sqrt(2.0 / math.pi)
GELU_B = GELU_A * 0.044715


def held(x):
    return pltpu.with_memory_space_constraint(x, pltpu.VMEM)


def stored(x):
    return pltpu.with_memory_space_constraint(x, pltpu.HBM)


WHOLE = pl.BlockSpec(memory_space=VM)


def product_weights(height, rows, mixing, w_ref, m_ref):
    inner, depth = 12 * height, 12 * height + 32
    k = lax.broadcasted_iota(jnp.int32, (depth, LANES), 0)
    j = lax.broadcasted_iota(jnp.int32, (depth, LANES), 1)
    bits = height.bit_length() - 1
    b, f, row = k >> (bits + 2), (k >> bits) & 3, k & (height - 1)
    edge = k - inner
    edge_b, below, edge_f = edge >> 3, (edge >> 2) & 1, edge & 3
    lanes = lax.broadcasted_iota(jnp.int32, (HID, LANES), 1)
    linear = jnp.zeros((depth, LANES), F32)
    width = FIELDS * height
    for r in range(height):
        inside = jnp.where(jnp.abs(row - r) <= 1, (3 * (row - r + 1) + b) * 4 + f, -1)
        border = (below * 6 + edge_b) * 4 + edge_f
        border = jnp.where(below * (height - 1) == r, border, -1)
        want = jnp.where(k < inner, inside, jnp.where(edge < 24, border, edge + 12))
        chosen = jnp.where(j == want, 1.0, 0.0).astype(BF)
        part = jnp.dot(chosen, rows, preferred_element_type=F32).astype(BF)
        w_ref[:, r * HID : (r + 1) * HID] = part
        spread = jnp.zeros((HID, LANES), F32)
        for field in range(FIELDS):
            spread = jnp.where(lanes == field * height + r, mixing[:, field : field + 1], spread)
        spread = spread.astype(BF)
        m_ref[r * HID : (r + 1) * HID, :] = spread[:, :width]
        linear = linear + jnp.dot(part, spread, preferred_element_type=F32)
    linear = linear[:, :width]
    coarse = linear.astype(BF)
    fine = (linear - coarse.astype(F32)).astype(BF)
    w_ref[:, height * HID : height * HID + 2 * width] = jnp.concatenate([coarse, fine], axis=1)


def weights_body(
    stencil_ref,
    offset_ref,
    mixing_ref,
    transform_ref,
    mean_ref,
    w_ref,
    m_ref,
    hw_ref,
    hm_ref,
    u_ref,
    rows_ref,
):
    rows_ref[...] = jnp.zeros_like(rows_ref)
    rows_ref[:36, :] = 0.5 * stencil_ref[...].astype(F32)
    rows = rows_ref[...]
    rest = 0.5 * offset_ref[...]
    for i in range(3):
        cut = rest.astype(BF).astype(F32)
        rest = rest - cut
        rows = jnp.where(lax.broadcasted_iota(jnp.int32, rows.shape, 0) == 36 + i, cut, rows)
    mixing = mixing_ref[...].astype(F32)
    mixing = jnp.concatenate([mixing, jnp.zeros((LANES - FIELDS, HID), F32)], axis=0).T
    product_weights(GROUP, rows.astype(BF), mixing, w_ref, m_ref)
    product_weights(8, rows.astype(BF), mixing, hw_ref, hm_ref)
    wide = jnp.concatenate([transform_ref[...], jnp.zeros((64, 64), F32)], axis=1)
    turned = jnp.concatenate([wide, jnp.zeros((64, LANES), F32)], axis=0).T[:64, :64]
    update = turned + mean_ref[...]
    update = update + (1.0 - jnp.sum(update, axis=1, keepdims=True)) * (1.0 / 64)
    coarse = update.astype(BF)
    u_ref[:64, :] = coarse
    u_ref[64:, :] = (update - coarse.astype(F32)).astype(BF)


def all_weights(stencil, offset, mixing, transform, mean_weights):
    return pl.pallas_call(
        weights_body,
        out_shape=(
            pltpu.HBM((DEPTH, GROUP * HID + LANES), BF),
            pltpu.HBM((GROUP * HID, 64), BF),
            pltpu.HBM((HOME_DEPTH, 8 * HID + LANES), BF),
            pltpu.HBM((8 * HID, 32), BF),
            pltpu.HBM((LANES, 64), BF),
        ),
        in_specs=[WHOLE] * 5,
        out_specs=(WHOLE,) * 5,
        scratch_shapes=[VM((LANES, HID), F32)],
        compiler_params=LIMIT,
        name="weights",
    )(*map(stored, (stencil.T, offset[None], mixing, transform, mean_weights[None])))


def forecast_body(chunks, columns, raw, edge_ref, w_ref, mix_ref, x_ref, *refs):
    o_ref, pa, pb, va, vb, ha, hb, s_ref, window_ref, w_held, mix_held, sems = refs
    copies = [
        pltpu.make_async_copy(
            x_ref.at[:, :, :, c * LANES : (c + 1) * LANES], window_ref.at[i], sems.at[i]
        )
        for i, c in enumerate(columns)
    ]
    late = weight_copies(w_ref, mix_ref, w_held, mix_held, sems, len(columns))
    for copy in copies + late:
        copy.start()
    for copy in copies:
        copy.wait()
    windows = {c: window_ref.at[i] for i, c in enumerate(columns)}
    for slot, c in enumerate(chunks):
        forecast_block(
            c,
            slot,
            windows,
            raw,
            late if slot == 0 else [],
            edge_ref,
            w_held,
            mix_held,
            o_ref,
            pa,
            pb,
            va,
            vb,
            ha,
            hb,
            s_ref,
        )


def weight_copies(w_ref, mix_ref, w_held, mix_held, sems, at):
    return [
        pltpu.make_async_copy(w_ref, w_held, sems.at[at]),
        pltpu.make_async_copy(mix_ref, mix_held, sems.at[at + 1]),
    ]


def forecast_block(
    c,
    slot,
    windows,
    raw,
    late,
    edge_ref,
    w_ref,
    mix_ref,
    o_ref,
    pa,
    pb,
    va,
    vb,
    ha,
    hb,
    s_ref,
):
    lane = lax.broadcasted_iota(jnp.int32, (1, LANES), 1)
    row8 = lax.broadcasted_iota(jnp.int32, (8, LANES), 0)
    ones = jnp.where(row8 < 3, 1.0, 0.0).astype(F32)

    def three(read):
        mid = read(c)
        left = read(c - 1) if c > 0 else jnp.zeros_like(mid)
        right = read(c + 1) if c < CHUNKS - 1 else jnp.zeros_like(mid)
        last = LANES - 1
        return (
            pltpu.roll(jnp.where(lane == last, left, mid), 1, 1),
            mid,
            pltpu.roll(jnp.where(lane == 0, right, mid), last, 1),
        )

    def block(k, f, g, cc):
        rows = pl.ds(pl.multiple_of(g * GROUP, GROUP), GROUP)
        return windows[cc][k, f, rows, :].astype(F32)

    def border(k, g, cc):
        out = edge_ref[k, :, cc * LANES : (cc + 1) * LANES]
        above, below = jnp.maximum(g - 1, 0), jnp.minimum(g + 1, GROUPS - 1)
        for f in range(FIELDS):
            up = pltpu.roll(block(k, f, above, cc)[8:], (f + 1) % 8, 0)
            down = pltpu.roll(block(k, f, below, cc)[:8], 4 + f, 0)
            out = jnp.where((row8 == f) & (g > 0), up, out)
            out = jnp.where((row8 == 4 + f) & (g < GROUPS - 1), down, out)
        return out

    def build(g, k, to):
        inner = [three(lambda cc: block(k, f, g, cc)) for f in range(FIELDS)]
        parts = [inner[f][b] for b in range(3) for f in range(FIELDS)]
        parts += [*three(lambda cc: border(k, g, cc)), ones]
        to[k * LANES : (k + 1) * LANES, :] = jnp.concatenate(parts, axis=0).astype(BF).T

    def pack(g, k, part):
        last = CHUNKS - 1
        here = slice(part * 8, part * 8 + 8)
        above, below = jnp.maximum(g - 1, 0), jnp.minimum(g + 1, GROUPS - 1)

        def outer(cc):
            out = edge_ref[k, :, cc * LANES : (cc + 1) * LANES]
            for f in range(FIELDS):
                inner = block(k, f, g, cc)
                up = inner[:8] if part else block(k, f, above, cc)[8:]
                down = block(k, f, below, cc)[:8] if part else inner[8:]
                out = jnp.where((row8 == f) & (part + g > 0), pltpu.roll(up, (f + 1) % 8, 0), out)
                use = (row8 == 4 + f) & (g + part < GROUPS)
                out = jnp.where(use, pltpu.roll(down, 4 + f, 0), out)
            return out

        main = [block(k, f, g, last)[here] for f in range(FIELDS)]
        left = [block(k, f, g, last - 1)[here] for f in range(FIELDS)] + [outer(last - 1)]
        column = jnp.zeros((8, LANES), F32)
        for n, v in enumerate(left):
            column = jnp.where(lane == n, pltpu.roll(v, n + 1, 1), column)
        main += [outer(last), column]
        for i in range(3):
            o_ref[2 * g + part, 256 + k * RAW + i * 16 : 272 + k * RAW + i * 16, :] = (
                jnp.concatenate(main[2 * i : 2 * i + 2], axis=0).astype(BF)
            )

    tiles = GROUP * HID // TILE
    held_v, held_h = (va, vb), (ha, hb)

    def group(g, patches, following, to):
        def before(n):
            held_v[n % 2][...] = jnp.dot(
                patches[...], w_ref[:, n * TILE : (n + 1) * TILE], preferred_element_type=F32
            ).astype(BF)

        linear = jnp.dot(patches[...], w_ref[:, GROUP * HID :], preferred_element_type=F32)
        total = linear[:, :64] + linear[:, 64:]
        before(0)
        for n in range(tiles + 1):
            if n + 1 < tiles:
                before(n + 1)
            if n < tiles:
                h = held_v[n % 2][...]
                bend = jnp.tanh(h * (h * h * BF(8 * GELU_B) + BF(2 * GELU_A)))
                held_h[n % 2][...] = h * bend
                build(following, n, to)
                if raw:
                    pack(g, n, 0)
                    pack(g, n, 1)
            if n >= 1:
                total = total + jnp.dot(
                    held_h[(n - 1) % 2][...],
                    mix_ref[(n - 1) * TILE : n * TILE, :],
                    preferred_element_type=F32,
                )
        moved = total.T
        rows = pl.ds(pl.multiple_of(g * GROUP, GROUP), GROUP)
        for k in range(MEMBERS):
            new = [
                windows[c][k, f, rows, :].astype(F32)
                + moved[f * GROUP : (f + 1) * GROUP, k * LANES : (k + 1) * LANES]
                for f in range(FIELDS)
            ]
            for f in range(FIELDS):
                for part in range(2):
                    at = pl.ds(f * 64 + k, 8, stride=8)
                    s_ref[part, at, :] = new[f][part * 8 : part * 8 + 8]
        for part in range(2):
            o_ref[2 * g + part, slot * 256 : slot * 256 + 256, :] = s_ref[part].astype(BF)

    for k in range(MEMBERS):
        build(0, k, pa)
    for copy in late:
        copy.wait()

    def step(i, _):
        group(2 * i, pa, 2 * i + 1, pb)
        group(2 * i + 1, pb, jnp.minimum(2 * i + 2, GROUPS - 1), pa)
        return 0

    lax.fori_loop(0, GROUPS // 2, step, 0)


def forecast_chunks(chunks, raw, x, edges, weights, mix):
    cells = MEMBERS * LANES
    count = len(chunks)
    low, high = chunks[0] - 1, CHUNKS - 1 if raw else chunks[-1] + 1
    columns = [c for c in range(CHUNKS) if low <= c <= high]
    window = (len(columns), MEMBERS, FIELDS, ROWS, LANES)
    shape = (8, count * 256 + raw * MEMBERS * RAW, LANES)
    return pl.pallas_call(
        functools.partial(forecast_body, chunks, columns, raw),
        grid=(1,),
        out_shape=jax.ShapeDtypeStruct(shape, BF),
        in_specs=[WHOLE] + [pl.BlockSpec(memory_space=pl.ANY)] * 3,
        out_specs=pl.BlockSpec(shape, lambda i: (0, 0, 0)),
        scratch_shapes=[VM((cells, DEPTH), BF)] * 2
        + [VM((cells, TILE), BF)] * 4
        + [VM((2, 256, LANES), F32), VM(window, BF)]
        + [VM(weights.shape, BF), VM(mix.shape, BF)]
        + [pltpu.SemaphoreType.DMA((len(columns) + 2,))],
        cost_estimate=pl.CostEstimate(
            flops=count * 10_000_000_000, bytes_accessed=4_000_000, transcendentals=0
        ),
        compiler_params=LIMIT,
        name=f"forecast_{chunks[0]}",
    )(edges, stored(weights), stored(mix), stored(x))


def home_body(
    x_ref, w_given, mix_given, o_ref, pa, pb, va, vb, ha, hb, s_ref, w_ref, mix_ref, sems
):
    late = weight_copies(w_given, mix_given, w_ref, mix_ref, sems, 0)
    for copy in late:
        copy.start()
    lane = lax.broadcasted_iota(jnp.int32, (1, LANES), 1)
    row8 = lax.broadcasted_iota(jnp.int32, (8, LANES), 0)
    ones = jnp.where(row8 < 3, 1.0, 0.0).astype(F32)
    last = LANES - 1

    def raw(m, k):
        got = [x_ref[m, 256 + k * RAW + i * 16 : 272 + k * RAW + i * 16, :] for i in range(3)]
        got = [v.astype(F32) for v in got]
        return [got[i // 2][i % 2 * 8 : i % 2 * 8 + 8] for i in range(6)]

    def build(m, k, to):
        *blocks, column = raw(m, k)
        three = []
        for n, mid in enumerate(blocks):
            first = pltpu.roll(column, (LANES - n) % LANES, 1)
            three.append(
                (
                    jnp.where(lane == 0, first, pltpu.roll(mid, 1, 1)),
                    mid,
                    jnp.where(lane == last, 0.0, pltpu.roll(mid, last, 1)),
                )
            )
        parts = [three[f][b] for b in range(3) for f in range(FIELDS)]
        parts += [*three[FIELDS], ones]
        to[k * LANES : (k + 1) * LANES, :] = jnp.concatenate(parts, axis=0).astype(BF).T

    tiles = 8 * HID // TILE
    held_v, held_h = (va, vb), (ha, hb)

    def group(m, patches, following, to):
        def before(n):
            held_v[n % 2][...] = jnp.dot(
                patches[...], w_ref[:, n * TILE : (n + 1) * TILE], preferred_element_type=F32
            ).astype(BF)

        linear = jnp.dot(patches[...], w_ref[:, 8 * HID :], preferred_element_type=F32)
        total = linear[:, :32] + linear[:, 32:64]
        before(0)
        for n in range(tiles + 1):
            if n + 1 < tiles:
                before(n + 1)
            if n < tiles:
                h = held_v[n % 2][...]
                bend = jnp.tanh(h * (h * h * BF(8 * GELU_B) + BF(2 * GELU_A)))
                held_h[n % 2][...] = h * bend
                build(following, 2 * n, to)
                build(following, 2 * n + 1, to)
            if n >= 1:
                total = total + jnp.dot(
                    held_h[(n - 1) % 2][...],
                    mix_ref[(n - 1) * TILE : n * TILE, :],
                    preferred_element_type=F32,
                )
        moved = total.T
        for k in range(MEMBERS):
            main = raw(m, k)
            for f in range(FIELDS):
                s_ref[pl.ds(f * 64 + k, 8, stride=8), :] = (
                    main[f] + moved[f * 8 : f * 8 + 8, k * LANES : (k + 1) * LANES]
                )
        o_ref[m] = s_ref[...].astype(BF)

    for k in range(MEMBERS):
        build(0, k, pa)
    for copy in late:
        copy.wait()

    def step(i, _):
        group(2 * i, pa, 2 * i + 1, pb)
        group(2 * i + 1, pb, jnp.minimum(2 * i + 2, 7), pa)
        return 0

    lax.fori_loop(0, 4, step, 0)


def home_forecast(states, weights, mix):
    cells = MEMBERS * LANES
    return pl.pallas_call(
        home_body,
        out_shape=jax.ShapeDtypeStruct((8, 256, LANES), BF),
        in_specs=[WHOLE] + [pl.BlockSpec(memory_space=pl.ANY)] * 2,
        out_specs=WHOLE,
        scratch_shapes=[VM((cells, HOME_DEPTH), BF)] * 2
        + [VM((cells, TILE), BF)] * 4
        + [VM((256, LANES), F32), VM(weights.shape, BF), VM(mix.shape, BF)]
        + [pltpu.SemaphoreType.DMA((2,))],
        cost_estimate=pl.CostEstimate(
            flops=10_000_000_000, bytes_accessed=4_000_000, transcendentals=0
        ),
        compiler_params=LIMIT,
        name="home",
    )(held(states), stored(weights), stored(mix))


def analysis_body(count, slots, a_ref, *refs):
    o_ref = refs[-1]
    for n in range(count):
        f_ref, slot = refs[n], slots[n]
        for q in range(4):
            spans = [slice((q * 8 + 2 * i) * 8, (q * 8 + 2 * i) * 8 + 16) for i in range(4)]
            got = [
                [f_ref[m, slot * 256 + span.start : slot * 256 + span.stop, :] for m in range(8)]
                for span in spans
            ]
            got = [[v.astype(F32) for v in vs] for vs in got]
            rows = [
                jnp.concatenate([v[h * 8 : h * 8 + 8] for v in got[i]], axis=0)
                for i in range(4)
                for h in range(2)
            ]
            states = jnp.concatenate(rows, axis=1).astype(BF)
            both = jnp.dot(a_ref[...], states, preferred_element_type=F32)
            total = both[:64] + both[64:]
            for i, span in enumerate(spans):
                for m in range(8):
                    pair = [
                        total[m * 8 : m * 8 + 8, (2 * i + h) * LANES : (2 * i + h + 1) * LANES]
                        for h in range(2)
                    ]
                    o_ref[m, n, span, :] = jnp.concatenate(pair, axis=0).astype(BF)


def analysis_chunks(update, states, slots, buffer, to, total):
    count = len(slots)
    given = [update, *[held(s) for s in states]]
    alias = {}
    if buffer is not None:
        alias = {len(given): 0}
        given.append(buffer)
    return pl.pallas_call(
        functools.partial(analysis_body, count, slots),
        grid=(1,),
        out_shape=pltpu.HBM((8, total, 256, LANES), BF),
        in_specs=[WHOLE] * (1 + count) + [pl.BlockSpec(memory_space=pl.ANY)] * len(alias),
        out_specs=pl.BlockSpec((8, count, 256, LANES), lambda i: (0, to // count, 0, 0)),
        input_output_aliases=alias,
        compiler_params=LIMIT,
        name=f"analysis_{to}",
    )(*given)


def observed_rows(index_ref, chunks, g_ref):
    for j in range(16):
        place = index_ref[j]
        p = lax.div(place, 4)
        odd = lax.rem(p, 2) == 1
        for c, (ref, slot) in chunks.items():

            @pl.when(lax.rem(place, 4) == c)
            def _():
                rows = pl.ds(pl.multiple_of(slot * 256 + lax.div(p, 2) * 16, 16), 16)
                for m in range(8):
                    two = ref[m, rows, :].astype(F32)
                    g_ref[m * 8 : m * 8 + 8, j * LANES : (j + 1) * LANES] = jnp.where(
                        odd, two[8:], two[:8]
                    )


def in_two(v):
    coarse = v.astype(BF)
    return coarse, (v - coarse.astype(F32)).astype(BF)


def gram_body(where, index_ref, values_ref, precision_ref, *refs):
    o_ref, g_ref = refs[-2:]
    observed_rows(index_ref, {c: (refs[i], slot) for c, i, slot in where}, g_ref)
    observed = g_ref[...]
    mean = jnp.sum(observed, axis=0, keepdims=True) * (1.0 / 64)
    spread = observed - mean
    weight = jnp.concatenate([precision_ref[j : j + 1, :] for j in range(16)], axis=1)
    value = jnp.concatenate([values_ref[j : j + 1, :] for j in range(16)], axis=1)
    left = jnp.broadcast_to(weight * (value - mean), (8, 2048))
    left = jnp.concatenate([spread * weight, left], axis=0)
    left, left_rest = in_two(left)
    right, right_rest = in_two(spread)
    both = lax.dot_general(
        jnp.concatenate([left, left, left_rest], axis=1),
        jnp.concatenate([right, right_rest, right], axis=1),
        (((1,), (1,)), ((), ())),
        preferred_element_type=F32,
    )
    gram, proj = both[:64], both[64:]
    for n in range(8):
        o_ref[n, 0:32, 0:64] = gram[:32]
        o_ref[n, 0:32, 64:128] = gram[32:]
        o_ref[n, 32:40, 0:64] = proj
        o_ref[n, 32:40, 64:128] = proj


def gram_part(index, values, precision, where, sources):
    return pl.pallas_call(
        functools.partial(gram_body, where),
        out_shape=jax.ShapeDtypeStruct((8, 40, LANES), F32),
        in_specs=[pl.BlockSpec(memory_space=pltpu.SMEM)] + [WHOLE] * (2 + len(sources)),
        out_specs=WHOLE,
        scratch_shapes=[VM((64, 2048), F32)],
        compiler_params=LIMIT,
        name="gram",
    )(index, values, precision, *[held(s) for s in sources])


def place_body(b_ref, near_ref, far_ref, o_ref, gram_ref, proj_ref, s_ref):
    for c in range(CHUNKS):
        for m in range(8):
            s_ref[m] = b_ref[m, c].astype(F32)
        for k in range(MEMBERS):
            for f in range(FIELDS):
                at = pl.ds(f * 64 + k, 8, stride=8)
                for half in range(4):
                    both = [s_ref[2 * half, at, :], s_ref[2 * half + 1, at, :]]
                    o_ref[
                        k, f, half * 16 : half * 16 + 16, c * LANES : (c + 1) * LANES
                    ] = jnp.concatenate(both, axis=0).astype(BF)
    total = near_ref[...] + far_ref[...]
    gram_ref[:32, :] = total[:32, :64] * (1.0 / OBSERVED)
    gram_ref[32:, :] = total[:32, 64:] * (1.0 / OBSERVED)
    proj_ref[...] = total[32:33, :64] * (1.0 / math.sqrt(OBSERVED))


def place(back, near, far):
    return pl.pallas_call(
        place_body,
        out_shape=(
            jax.ShapeDtypeStruct((MEMBERS, FIELDS, ROWS, COLS), BF),
            jax.ShapeDtypeStruct((64, 64), F32),
            jax.ShapeDtypeStruct((1, 64), F32),
        ),
        in_specs=[WHOLE] * 3,
        out_specs=(WHOLE,) * 3,
        scratch_shapes=[VM((8, 256, LANES), F32)],
        compiler_params=LIMIT,
        name="place",
    )(held(back), near, far)


def sum_over(part, axis, steps):
    size = lax.axis_size(axis)
    got = [lax.ppermute(part, axis, [(i, step(i)) for i in range(size)]) for step in steps]
    return functools.reduce(lambda a, b: a + b, got, part)


def shards(
    prior_realizations,
    latent_stencil_weights,
    latent_offset,
    output_mixing_matrix,
    transform,
    mean_weights,
    obs_index,
    obs_values,
    obs_precision,
):
    count = lax.axis_size("state")
    forward = [(i, i + 1) for i in range(count - 1)]
    backward = [(i + 1, i) for i in range(count - 1)]
    low = lax.ppermute(prior_realizations[:, :, ROWS - 1, :], "state", forward)
    high = lax.ppermute(prior_realizations[:, :, 0, :], "state", backward)
    edges = jnp.concatenate([low, high], axis=1).astype(F32)

    weights, mix, home_weights, home_mix, update = all_weights(
        latent_stencil_weights, latent_offset, output_mixing_matrix, transform, mean_weights
    )
    index = obs_index[0, 0]

    exchange = functools.partial(
        lax.all_to_all, axis_name="mem", split_axis=0, concat_axis=0, tiled=True
    )

    def forecast(chunks, raw):
        return forecast_chunks(chunks, raw, prior_realizations, edges, weights, mix)

    x0 = exchange(forecast((0,), True))
    x1 = exchange(forecast((1, 2), False))
    x2 = home_forecast(x0, home_weights, home_mix)
    part = gram_part(
        index,
        obs_values[0, 0],
        obs_precision[0, 0],
        [(0, 0, 0), (1, 1, 0), (2, 1, 1), (3, 2, 0)],
        [x0, x1, x2],
    )
    total = jnp.sum(exchange(part), axis=0)
    held4 = analysis_chunks(update, [x0, x1, x1, x2], [0, 0, 1, 0], None, 0, 4)
    held4, total = lax.optimization_barrier((held4, total))
    x4 = exchange(held4)
    for n in (1, 2, 4, 8):
        total = sum_over(total, "state", [lambda i, n=n: i ^ n])
    far = lax.ppermute(total, "state", [(i, i ^ 16) for i in range(count)])
    analysis, gram, proj = place(x4, total, far)
    return (analysis, gram, proj.reshape(64))


def solution(mesh):
    return jax.shard_map(
        shards,
        mesh=mesh,
        in_specs=(
            P("mem", None, "state", None),
            P(),
            P(),
            P(),
            P(),
            P(),
            P("state", "mem", None),
            P("state", "mem", None, None),
            P("state", "mem", None, None),
        ),
        out_specs=(P("mem", None, "state", None), P(), P()),
        check_vma=False,
    )
```
